128 devices in a mesh: gx: 16 (over z, x_hi, core), gy: 8 (over x_lo, y).
Axes of the slice: x: 4 (x_hi: 2, x_lo: 2; x = x_hi * 2 + x_lo), y: 4, z: 4, core: 2. Of those that a mesh axis runs over, the one named last changes fastest.
Arguments:
- kpot: float32 [2, 16, 1024, 1024], P(None, 'gy', 'gx'), may hold values from -6144 to 6144
- atom_cell: int32 [16384, 2], P(('gx', 'gy')), may hold values from 0 to 1023, as said below
- expo: int32 [16384, 64], P(('gx', 'gy')), may hold values from 0 to 11
- pair_atoms: int32 [16384, 2], P(('gx', 'gy')), may hold values from 0 to 127, as said below
- pair_block: int32 [16384], P(('gx', 'gy')), may hold values from 0 to 127
- block_slot: int32 [128], replicated, may hold values from 0 to 127, each once
Outputs:
- potential: float32 [16, 1024, 1024], P('gy', None, 'gx')
- blocks: float32 [128, 64, 64], P(('gx', 'gy'))
The draws below stay inside these ranges and needn't reach their ends.
Inputs may be any that keep to these rules, and one draw needn't show every extreme that they name: `atom_cell`: atoms come in groups of four consecutive ones whose centres lie within 8 cells of a common point. `pair_atoms`: both atoms of an entry are in the same group of four.
All inputs are finite; a program needn't handle non-finite values.
Results may differ from the reference program's by a relative error of at most 0.0003.
Values sent between devices are 32-bit elements; how exact they have to be, the bound alone decides.
A program may use at most 64 MiB of HBM per device.

```python
import jax
import jax.numpy as jnp
from jax import lax

NX = 1024
NY = 1024
PL_DEV = 2
NB = 64
W = 32
NE = 12
A_DEV = 128
PAIRS_DEV = 128
P_SIZE = 16
CXL = 64
N_ATOMS = 16384
N_PAIRS = 16384
N_BLOCKS = 128
N_GX = 16
N_GY = 8


def draw_atom_cell(key, part):
    groups = N_ATOMS // 4
    keys = jax.random.split(key, 4)
    centre_y = jax.random.randint(keys[0], (groups,), 0, NY)
    centre_x = jax.random.randint(keys[1], (groups,), 0, CXL)
    off_y = jax.random.randint(keys[2], (groups, 4), -(W // 4), W // 4 + 1)
    off_x = jax.random.randint(keys[3], (groups, 4), -(W // 4), W // 4 + 1)
    cell_y = (centre_y[:, None] + off_y) % NY
    cell_x = jnp.clip(centre_x[:, None] + off_x, 0, CXL - 1)
    return jnp.stack([cell_y.reshape(-1), cell_x.reshape(-1)], axis=1).astype(jnp.int32)


def draw_pair_atoms(key, part):
    keys = jax.random.split(jax.random.fold_in(key, 7), 2)
    first = jax.random.randint(keys[0], (N_PAIRS,), 0, A_DEV)
    second = 4 * (first // 4) + jax.random.randint(keys[1], (N_PAIRS,), 0, 4)
    return jnp.stack([first, second], axis=1).astype(jnp.int32)


def set_ends(values, key, smallest, high):
    longest = values.shape.index(max(values.shape))
    spots = []
    for shift in (0, 1):
        where = [jax.random.randint(jax.random.fold_in(key, axis), (), 0, length) for axis, length in enumerate(values.shape)]
        where[longest] = (where[longest] + shift) % values.shape[longest]
        spots.append(tuple(where))
    return values.at[spots[0]].set(smallest).at[spots[1]].set(high)


def level_of(stream_key, extent, cuts, smallest, high):
    gain, own = 1.0, jax.random.fold_in(stream_key, 6)
    for axis_at, blocks in cuts:
        steps = jnp.exp(jax.random.uniform(jax.random.fold_in(own, axis_at), (blocks,), jnp.float32, smallest / len(cuts), high / len(cuts)))
        gain = gain * jnp.repeat(steps, extent[axis_at] // blocks).reshape([-1 if axis == axis_at else 1 for axis in range(len(extent))])
    return gain


def noise(stream_key, shape, width, bound, cuts=(), dtype=jnp.bfloat16):
    drawn = width * jax.random.normal(stream_key, shape, jnp.float32)
    if cuts:
        drawn = drawn * level_of(stream_key, shape, cuts, -0.22, 0.18)
    return jnp.clip(drawn, -bound, bound).astype(dtype)


def setup_inputs(seed: int = 0) -> dict:
    arg_keys = jax.random.split(jax.random.key(seed), 7)
    return {
        "kpot": noise(arg_keys[0], (2, P_SIZE, NY, NX), NX, 6144.0, ((1, 8), (2, 16)), jnp.float32),
        "atom_cell": draw_atom_cell(jax.random.fold_in(arg_keys[6], 71), 0),
        "expo": set_ends(jax.random.randint(arg_keys[2], (N_ATOMS, NB), 0, NE), jax.random.fold_in(arg_keys[2], 1), 0, NE - 1).astype(jnp.int32),
        "pair_atoms": draw_pair_atoms(jax.random.fold_in(arg_keys[6], 71), 0),
        "pair_block": set_ends(jax.random.randint(arg_keys[4], (N_PAIRS,), 0, N_BLOCKS), jax.random.fold_in(arg_keys[4], 1), 0, N_BLOCKS - 1).astype(jnp.int32),
        "block_slot": jax.random.permutation(arg_keys[5], N_BLOCKS).astype(jnp.int32),
    }


def alpha_table():
    steps = jnp.arange(NE).astype(jnp.float32)
    return (2.0 / (W * W)) * 16.0 ** (steps / (NE - 1))


def lookup(exps, table):
    hits = exps[:, None] == jnp.arange(NE)[None, :]
    return jnp.sum(jnp.where(hits, table[None, :], jnp.zeros_like(table)[None, :]), axis=1)


def radius(shift_y, shift_x):
    offs = (jnp.arange(W) - W // 2).astype(jnp.float32)
    depth = jnp.arange(PL_DEV).astype(jnp.float32) - (PL_DEV - 1) / 2.0
    along_y = offs + shift_y.astype(jnp.float32)
    along_x = offs + shift_x.astype(jnp.float32)
    full = depth[:, None, None] ** 2 + along_y[None, :, None] ** 2 + along_x[None, None, :] ** 2
    return full.reshape(-1)


def reference(kpot, atom_cell, expo, pair_atoms, pair_block, block_slot):
    spec = kpot[0] + 1j * kpot[1]
    potential = jnp.real(jnp.fft.ifft2(spec, axes=(1, 2)))
    table = alpha_table()
    offs = jnp.arange(W) - W // 2
    devices = N_GX * N_GY
    zero = jnp.zeros((), jnp.int32)

    def device_term(total, dev):
        ix = dev // N_GY
        iy = dev % N_GY
        planes = lax.dynamic_slice_in_dim(potential, (iy * PL_DEV).astype(jnp.int32), PL_DEV, 0)
        cells = lax.dynamic_slice(atom_cell, ((dev * A_DEV).astype(jnp.int32), zero), (A_DEV, 2))
        exps = lax.dynamic_slice(expo, ((dev * A_DEV).astype(jnp.int32), zero), (A_DEV, NB))
        pairs = lax.dynamic_slice(pair_atoms, ((dev * PAIRS_DEV).astype(jnp.int32), zero), (PAIRS_DEV, 2))
        ids = lax.dynamic_slice_in_dim(pair_block, (dev * PAIRS_DEV).astype(jnp.int32), PAIRS_DEV, 0)

        def one(pair):
            first = cells[pair[0]]
            second = cells[pair[1]]
            rows = (first[0] + offs) % NY
            cols = (ix * CXL + first[1] + offs) % NX
            window = planes[:, rows][:, :, cols].reshape(-1)
            shift_y = (first[0] - second[0] + NY // 2) % NY - NY // 2
            shift_x = first[1] - second[1]
            alpha_i = lookup(exps[pair[0]], table)
            alpha_j = lookup(exps[pair[1]], table)
            phi_i = jnp.exp(-alpha_i[:, None] * radius(zero, zero)[None, :])
            phi_j = jnp.exp(-alpha_j[:, None] * radius(shift_y, shift_x)[None, :])
            entry = jnp.dot(phi_i * window[None, :], phi_j.T, precision=lax.Precision.HIGHEST)
            return (entry / W).reshape(-1)

        entries = lax.map(one, pairs)
        slots = block_slot[ids]
        return total + jax.ops.segment_sum(entries, slots, N_BLOCKS), None

    start = jnp.zeros((N_BLOCKS, NB * NB), jnp.float32)
    total, unused = lax.scan(device_term, start, jnp.arange(devices).astype(jnp.int32))
    return potential, total.reshape(N_BLOCKS, NB, NB)
```

```python
import math

import jax
import jax.numpy as jnp
import ml_dtypes
import numpy as np
from jax import lax
from jax.experimental import pallas as pl
from jax.experimental.pallas import tpu as pltpu
from jax.sharding import PartitionSpec as P

W = 32
NE = 12
ROWS = NE * NE
SPAN = 33
N = 1024
R = 4
M = N // R
CXL = 64
MESH = pl.DeviceIdType.MESH
NT = (((1,), (1,)), ((), ()))
F32 = jnp.float32
BF16 = jnp.bfloat16


def split_np(values):
    high = values.astype(np.float32).astype(ml_dtypes.bfloat16)
    low = (values - high.astype(np.float64)).astype(np.float32).astype(ml_dtypes.bfloat16)
    return high, low


def split(values):
    high = values.astype(BF16)
    low = (values - high.astype(F32)).astype(BF16)
    return high, low


def transform_tables():
    n = np.arange(M)
    angle = 2.0 * math.pi / M * ((n[:, None] * n[None, :]) % M)
    cos, sin = np.cos(angle), np.sin(angle)
    tab1 = np.stack([*split_np(cos), *split_np(sin)])
    def spread(t):
        t = t.reshape(M, R, CXL)
        return np.stack([t, t], axis=2).reshape(M, 2 * M)

    tab2 = np.stack(split_np(np.concatenate([spread(cos), -spread(sin)], axis=1)))
    t = np.arange(R)
    turn = 2.0 * math.pi / N * (t[:, None] * n[None, :])
    tw1 = np.stack([np.cos(turn), np.sin(turn)], axis=1).astype(np.float32).reshape(2 * R, M)
    scale = 1.0 / (N * N)
    tw2 = np.stack([np.cos(turn), np.sin(turn)], axis=1) * scale
    tw2 = tw2.reshape(R, 2, R, 1, CXL)
    tw2 = np.broadcast_to(tw2, (R, 2, R, 2, CXL)).astype(np.float32).reshape(R * 2 * R, 2 * CXL)
    return tab1, tab2, tw1, tw2


def gauss_tables():
    alpha = (2.0 / (W * W)) * 16.0 ** (np.arange(NE) / (NE - 1))
    offs = np.arange(W) - W // 2
    shift = np.arange(SPAN) - SPAN // 2
    e = alpha[None, :, None, None] * (offs**2)[None, None, None, :]
    f = alpha[None, None, :, None] * ((offs[None, :] + shift[:, None]) ** 2)[:, None, None, :]
    grid = np.exp(-(e + f)).reshape(SPAN, ROWS, W)
    high, low = split_np(grid)
    first = np.concatenate([high, high, low, low], axis=2)
    depth = np.exp(-(alpha[:, None] + alpha[None, :]) * 0.25).reshape(1, ROWS, 1) / W
    second = np.tile((grid * depth).astype(np.float32), (1, 1, 4))
    return first, second


def butterfly(re, im):
    ar, br, cr, dr = re[0] + re[2], re[0] - re[2], re[1] + re[3], re[1] - re[3]
    ai, bi, ci, di = im[0] + im[2], im[0] - im[2], im[1] + im[3], im[1] - im[3]
    return (
        (ar + cr, ai + ci),
        (br - di, bi + dr),
        (ar - cr, ai - ci),
        (br + di, bi - dr),
    )


def transform_kernel(
    kpot, tab1, tab2, tw1, tw2, pot, padded,
    z1h, z1l, fsend, grecv, z2h, z2l, yx, send_sem, recv_sem, rim_send, rim_recv,
):
    me = lax.axis_index("gx")
    count = 16
    barrier = pltpu.get_barrier_semaphore()
    for k in range(1, count):
        pl.semaphore_signal(
            barrier, inc=1, device_id={"gx": lax.rem(me + k, count)}, device_id_type=MESH
        )

    for p in range(2):
        def rows_step(c, carry, p=p):
            row = pl.multiple_of(c * 16, 16)
            re = [kpot[0, p, pl.ds(row, 16), s * M:(s + 1) * M] for s in range(R)]
            im = [kpot[1, p, pl.ds(row, 16), s * M:(s + 1) * M] for s in range(R)]
            for t, (yr, yi) in enumerate(butterfly(re, im)):
                if t:
                    wr = tw1[2 * t:2 * t + 1, :]
                    wi = tw1[2 * t + 1:2 * t + 2, :]
                    yr, yi = yr * wr - yi * wi, yr * wi + yi * wr
                for c_at, part in enumerate((yr, yi)):
                    high, low = split(part)
                    at = pl.ds(pl.multiple_of(c_at * 128 + p * 64 + row, 16), 16)
                    z1h[t, at, :] = high
                    z1l[t, at, :] = low
            return carry
        lax.fori_loop(0, 4, rows_step, 0)

    for t in range(R):
        zh, zl = z1h[t], z1l[t]
        def three(at):
            out = lax.dot_general(tab1[at], zh, NT, preferred_element_type=F32)
            out += lax.dot_general(tab1[at], zl, NT, preferred_element_type=F32)
            out += lax.dot_general(tab1[at + 1], zh, NT, preferred_element_type=F32)
            return out
        cz = three(0)
        sz = three(2)
        fre = cz[:, :128] - sz[:, 128:]
        fim = sz[:, :128] + cz[:, 128:]
        for d in range(count):
            fsend[d, 0, pl.ds(t, 16, stride=R), :] = fre[d * 16:(d + 1) * 16]
            fsend[d, 1, pl.ds(t, 16, stride=R), :] = fim[d * 16:(d + 1) * 16]

    pl.semaphore_wait(barrier, count - 1)
    copies = []
    for k in (8, 7, 9, 6, 10, 5, 11, 4, 12, 3, 13, 2, 14, 15, 1):
        other = lax.rem(me + k, count)
        copy = pltpu.make_async_remote_copy(
            src_ref=fsend.at[other],
            dst_ref=grecv.at[me],
            send_sem=send_sem.at[k],
            recv_sem=recv_sem.at[k],
            device_id={"gx": other},
            device_id_type=MESH,
        )
        copy.start()
        copies.append(copy)
    grecv[me] = fsend[me]
    for copy in copies:
        copy.wait()

    lane = lax.broadcasted_iota(jnp.int32, (16, 128), 1)
    for j in range(R):
        def cells_step(c, carry, j=j):
            row = pl.multiple_of(c * 16, 16)
            re = [grecv[R * s + j, 0, pl.ds(row, 16), :] for s in range(R)]
            im = [grecv[R * s + j, 1, pl.ds(row, 16), :] for s in range(R)]
            for t, (yr, yi) in enumerate(butterfly(re, im)):
                base = t * 2 * R + j
                wr = tw2[base:base + 1, :]
                if t:
                    wi = tw2[base + R:base + R + 1, :]
                    yr, yi = yr * wr - yi * wi, yr * wi + yi * wr
                else:
                    yr, yi = yr * wr, yi * wr
                for c_at, part in enumerate((yr, yi)):
                    for p in range(2):
                        mine = jnp.where((lane >= 64) == (p == 1), part, 0.0)
                        high, low = split(mine)
                        at = pl.ds(pl.multiple_of(t * 128 + p * 64 + row, 16), 16)
                        cols = slice((c_at * R + j) * 128, (c_at * R + j + 1) * 128)
                        z2h[at, cols] = high
                        z2l[at, cols] = low
            return carry
        lax.fori_loop(0, 4, cells_step, 0)

    for half in range(2):
        zh = z2h[half * 256:(half + 1) * 256, :]
        zl = z2l[half * 256:(half + 1) * 256, :]
        out = lax.dot_general(tab2[0], zh, NT, preferred_element_type=F32)
        out += lax.dot_general(tab2[0], zl, NT, preferred_element_type=F32)
        out += lax.dot_general(tab2[1], zh, NT, preferred_element_type=F32)
        for i in range(2):
            yx[pl.ds(half * 2 + i, M, stride=R), :] = out[:, i * 128:(i + 1) * 128]
    for b in range(N // 128):
        tile = jnp.transpose(yx[b * 128:(b + 1) * 128, :])
        cols = slice(b * 128, (b + 1) * 128)
        pot[0, :, cols] = tile[:64]
        pot[1, :, cols] = tile[64:]
        total = tile[:64] + tile[64:]
        padded[b, 16:80, :] = total
        if b == 0:
            padded[N // 128, 16:80, :] = total

    left = lax.rem(me + count - 1, count)
    right = lax.rem(me + 1, count)
    to_left = pltpu.make_async_remote_copy(
        src_ref=padded.at[:, 16:32, :], dst_ref=padded.at[:, 80:96, :],
        send_sem=rim_send.at[0], recv_sem=rim_recv.at[0],
        device_id={"gx": left}, device_id_type=MESH,
    )
    to_right = pltpu.make_async_remote_copy(
        src_ref=padded.at[:, 64:80, :], dst_ref=padded.at[:, 0:16, :],
        send_sem=rim_send.at[1], recv_sem=rim_recv.at[1],
        device_id={"gx": right}, device_id_type=MESH,
    )
    to_left.start()
    to_right.start()
    to_left.wait()
    to_right.wait()


def pairs_kernel(
    cell_s, pair_s, padded, expo_t, pair_v, block_v, slot_v, first, second, out,
    table, xsel, ei, ej, ebuf,
):
    lane = lax.broadcasted_iota(jnp.int32, (W, 128), 1)
    lane_wide = lax.broadcasted_iota(jnp.int32, (ROWS, 128), 1)
    group_of_row = (lax.broadcasted_iota(jnp.int32, (256, 128), 0) >> 5) & 3
    column = lax.broadcasted_iota(jnp.int32, (256, 128), 1)
    table[...] = jnp.zeros_like(table)

    def group(g, carry):
        tabs, cells, seconds = [], [], []
        for q in range(4):
            i = pair_s[0, 4 * g + q]
            j = pair_s[1, 4 * g + q]
            cy, cx = cell_s[0, i], cell_s[1, i]
            dy = ((cy - cell_s[0, j] + N // 2) & (N - 1)) - N // 2
            dx = cx - cell_s[1, j]
            start = (cy - W // 2) & (N - 1)
            tile = start >> 7
            off = start & 127
            low_part = padded[tile, pl.ds(cx, W), :]
            high_part = padded[tile + 1, pl.ds(cx, W), :]
            turn = (32 * q - off) & 127
            low_part = pltpu.roll(low_part, turn, 1)
            high_part = pltpu.roll(high_part, turn, 1)
            window = jnp.where(lane < 128 + 32 * q - off, low_part, high_part)
            window = jnp.where((lane >> 5) == q, window, 0.0)
            high, low = split(window)
            cells += [high, low, high, low]
            tabs.append(first[dx + SPAN // 2])
            seconds.append(second[dy + SPAN // 2])
        t = jnp.dot(
            jnp.concatenate(tabs[:2], axis=1), jnp.concatenate(cells[:8], axis=0),
            preferred_element_type=F32,
        )
        t += jnp.dot(
            jnp.concatenate(tabs[2:], axis=1), jnp.concatenate(cells[8:], axis=0),
            preferred_element_type=F32,
        )
        other = jnp.where(
            lane_wide < 64,
            jnp.where(lane_wide < 32, seconds[0], seconds[1]),
            jnp.where(lane_wide < 96, seconds[2], seconds[3]),
        )
        high, low = split(t * other)
        ones = jnp.where(group_of_row + 4 * g == column, 1.0, 0.0).astype(BF16)
        table[...] += jnp.dot(
            jnp.concatenate([high, low], axis=1), ones, preferred_element_type=F32
        )
        return carry

    lax.fori_loop(0, 32, group, 0, unroll=2)

    sub = lax.broadcasted_iota(jnp.int32, (128, 128), 0)
    exps = expo_t[...].astype(F32).astype(BF16)
    for side, ref in ((0, ei), (1, ej)):
        hot = jnp.where(pair_v[side:side + 1, :] == sub, 1.0, 0.0).astype(BF16)
        ref[...] = jnp.dot(exps, hot, preferred_element_type=F32)

    def choose_second(c, carry):
        rows = pl.ds(pl.multiple_of(c * 16, 16), 16)
        mine = ej[rows, :]
        masks = [mine == float(f) for f in range(1, NE)]
        for e in range(NE):
            got = jnp.broadcast_to(table[e * NE:e * NE + 1, :], (16, 128))
            for f in range(1, NE):
                got = jnp.where(masks[f - 1], table[e * NE + f:e * NE + f + 1, :], got)
            xsel[e, rows, :] = got
        return carry

    lax.fori_loop(0, 4, choose_second, 0)

    for c in range(4):
        held = [xsel[e, c * 16:(c + 1) * 16, :] for e in range(NE)]

        def choose_first(k, carry, c=c, held=held):
            mine = jnp.broadcast_to(ei[pl.ds(k, 1), :], (16, 128))
            got = held[0]
            for e in range(1, NE):
                got = jnp.where(mine == float(e), held[e], got)
            high, low = split(got)
            at = pl.ds(pl.multiple_of(k * 64 + c * 16, 16), 16)
            ebuf[at, 0:128] = high
            ebuf[at, 128:256] = low
            return carry

        lax.fori_loop(0, 64, choose_first, 0, unroll=4)

    block_hot = jnp.where(block_v[...] == sub, 1.0, 0.0).astype(BF16)
    slot = slot_v[...]
    z, xh, core, xl, y = slot >> 5, (slot >> 4) & 1, (slot >> 3) & 1, (slot >> 2) & 1, slot & 3
    x = xh * 2 + xl
    for h in range(2):
        a, b = (y, z) if h == 0 else (z, y)
        place = core * 64 + a * 16 + b * 4 + x
        owner = jnp.where(place == sub, 1.0, 0.0).astype(BF16)
        hits = jnp.dot(owner, block_hot, preferred_element_type=F32).astype(BF16)
        hits = jnp.concatenate([hits, hits], axis=1)
        for c in range(4):
            at = h * 2048 + c * 512
            out[h, :, c * 512:(c + 1) * 512] = lax.dot_general(
                hits, ebuf[at:at + 512, :], NT, preferred_element_type=F32
            )


def reduce_kernel(
    part, out, ra, sb, rb, tb, rc, tc, rd,
    sa_sem, ra_sem, sb_sem, rb_sem, sc_sem, rc_sem, sd_sem, rd_sem,
):
    gx = lax.axis_index("gx")
    gy = lax.axis_index("gy")
    z, xh, core = gx // 4, lax.rem(gx // 2, 2), lax.rem(gx, 2)
    xl, y = gy // 4, lax.rem(gy, 4)
    x = xh * 2 + xl
    sibling = {"gx": z * 4 + xh * 2 + (1 - core), "gy": gy}

    def at_y(k):
        return {"gx": gx, "gy": xl * 4 + lax.rem(y + k, 4)}

    def at_z(k):
        return {"gx": lax.rem(z + k, 4) * 4 + xh * 2 + core, "gy": gy}

    def at_x(k):
        to = lax.rem(x + k, 4)
        return {"gx": z * 4 + (to // 2) * 2 + core, "gy": lax.rem(to, 2) * 4 + y}

    barrier = pltpu.get_barrier_semaphore()
    partners = [sibling] + [at(k) for at in (at_y, at_z, at_x) for k in (1, 2, 3)]
    for device in partners:
        pl.semaphore_signal(barrier, inc=1, device_id=device, device_id_type=MESH)
    pl.semaphore_wait(barrier, len(partners))

    def send(src, dst, ssem, rsem, device):
        copy = pltpu.make_async_remote_copy(
            src_ref=src, dst_ref=dst, send_sem=ssem, recv_sem=rsem,
            device_id=device, device_id_type=MESH,
        )
        copy.start()
        return copy

    order = (2, 1, 3, 0)
    mine = (y, z)
    then = (z, y)
    pending = []
    first = {}
    for k in order:
        for h in range(2):
            a = lax.rem(mine[h] + k, 4)
            first[h, k] = send(
                part.at[h, 1 - core, a], ra.at[h, k], sa_sem.at[h, k], ra_sem.at[h, k], sibling
            )
    second = {}
    for k in order:
        for h in range(2):
            a = lax.rem(mine[h] + k, 4)
            first[h, k].wait_recv()
            sb[h, k] = part[h, core, a] + ra[h, k]
            if k:
                device = at_y(k) if h == 0 else at_z(k)
                second[h, k] = send(
                    sb.at[h, k], rb.at[h, k], sb_sem.at[h, k], rb_sem.at[h, k], device
                )
    third = {}
    for h in range(2):
        for k in (1, 3, 2):
            second[h, k].wait_recv()
        total = sb[h, 0] + rb[h, 1] + rb[h, 2] + rb[h, 3]
        for c in range(16):
            tb[h, :, c, :] = total[:, c * 128:(c + 1) * 128]
        for k in (2, 1, 3):
            to = lax.rem(then[h] + k, 4)
            device = at_z(k) if h == 0 else at_y(k)
            third[h, k] = send(
                tb.at[h, pl.ds(to * 4, 4)], rc.at[h, k], sc_sem.at[h, k], rc_sem.at[h, k], device
            )
    fourth = {}
    for h in range(2):
        for k in (1, 3, 2):
            third[h, k].wait_recv()
        tc[h] = tb[h, pl.ds(then[h] * 4, 4)] + rc[h, 1] + rc[h, 2] + rc[h, 3]
        for k in (2, 1, 3):
            to = lax.rem(x + k, 4)
            fourth[h, k] = send(
                tc.at[h, to], rd.at[h, k], sd_sem.at[h, k], rd_sem.at[h, k], at_x(k)
            )
    for h in range(2):
        for k in (1, 3, 2):
            fourth[h, k].wait_recv()
        out[h] = tc[h, x] + rd[h, 1] + rd[h, 2] + rd[h, 3]
    for group in (first, second, third, fourth):
        for copy in group.values():
            copy.wait_send()


def body(kpot, atom_cell, expo, pair_atoms, pair_block, block_slot):
    vmem = pl.BlockSpec(memory_space=pltpu.VMEM)
    smem = pl.BlockSpec(memory_space=pltpu.SMEM)
    dma = pltpu.SemaphoreType.DMA
    tab1, tab2, tw1, tw2 = [jnp.asarray(t) for t in transform_tables()]
    first, second = [jnp.asarray(t) for t in gauss_tables()]
    potential, padded = pl.pallas_call(
        transform_kernel,
        out_shape=(
            jax.ShapeDtypeStruct((2, CXL, N), F32),
            jax.ShapeDtypeStruct((N // 128 + 1, 96, 128), F32),
        ),
        in_specs=[vmem] * 5,
        out_specs=(vmem, vmem),
        scratch_shapes=[
            pltpu.VMEM((R, 256, M), BF16),
            pltpu.VMEM((R, 256, M), BF16),
            pltpu.VMEM((16, 2, CXL, 128), F32),
            pltpu.VMEM((16, 2, CXL, 128), F32),
            pltpu.VMEM((512, N), BF16),
            pltpu.VMEM((512, N), BF16),
            pltpu.VMEM((N, 128), F32),
            dma((16,)), dma((16,)), dma((2,)), dma((2,)),
        ],
        compiler_params=pltpu.CompilerParams(
            collective_id=0, has_side_effects=True, vmem_limit_bytes=40 * 2**20
        ),
        name="transform",
    )(kpot, tab1, tab2, tw1, tw2)
    cell_t, pair_t = atom_cell.T, pair_atoms.T
    part = pl.pallas_call(
        pairs_kernel,
        out_shape=jax.ShapeDtypeStruct((2, 128, 2048), F32),
        in_specs=[smem, smem] + [vmem] * 7,
        out_specs=vmem,
        scratch_shapes=[
            pltpu.VMEM((ROWS, 128), F32),
            pltpu.VMEM((NE, 64, 128), F32),
            pltpu.VMEM((64, 128), F32),
            pltpu.VMEM((64, 128), F32),
            pltpu.VMEM((4096, 256), BF16),
        ],
        compiler_params=pltpu.CompilerParams(vmem_limit_bytes=40 * 2**20),
        name="pairs",
    )(
        cell_t, pair_t, padded, expo.T, pair_t,
        pair_block.reshape(1, -1), block_slot.reshape(1, -1), first, second,
    )
    own = pl.pallas_call(
        reduce_kernel,
        out_shape=jax.ShapeDtypeStruct((2, 16, 128), F32),
        in_specs=[vmem],
        out_specs=vmem,
        scratch_shapes=[
            pltpu.VMEM((2, 4, 16, 2048), F32),
            pltpu.VMEM((2, 4, 16, 2048), F32),
            pltpu.VMEM((2, 4, 16, 2048), F32),
            pltpu.VMEM((2, 16, 16, 128), F32),
            pltpu.VMEM((2, 4, 4, 16, 128), F32),
            pltpu.VMEM((2, 4, 16, 128), F32),
            pltpu.VMEM((2, 4, 16, 128), F32),
        ] + [dma((2, 4))] * 8,
        compiler_params=pltpu.CompilerParams(
            collective_id=1, has_side_effects=True, vmem_limit_bytes=40 * 2**20
        ),
        name="reduce",
    )(part.reshape(2, 2, 4, 16, 2048))
    return jnp.transpose(potential, (0, 2, 1)), own.reshape(1, 64, 64)


def solution(mesh):
    return jax.shard_map(
        body,
        mesh=mesh,
        in_specs=(
            P(None, "gy", "gx", None),
            P(("gx", "gy"), None),
            P(("gx", "gy"), None),
            P(("gx", "gy"), None),
            P(("gx", "gy")),
            P(),
        ),
        out_specs=(P("gy", None, "gx"), P(("gx", "gy"), None, None)),
        check_vma=False,
    )
```

```python
import math

import jax
import jax.numpy as jnp
import ml_dtypes
import numpy as np
from jax import lax
from jax.experimental import pallas as pl
from jax.experimental.pallas import tpu as pltpu
from jax.sharding import PartitionSpec as P

W = 32
NE = 12
ROWS = NE * NE
WIDE = 256
SPAN = 33
N = 1024
R = 4
M = N // R
CXL = 64
KS = (24, 24, 16)
STEP = 8
MSG = 280
BLOB = 4096
USED = 816
MESH = pl.DeviceIdType.MESH
NT = (((1,), (1,)), ((), ()))
F32 = jnp.float32
BF16 = jnp.bfloat16


def split_np(values):
    high = values.astype(np.float32).astype(ml_dtypes.bfloat16)
    low = (values - high.astype(np.float64)).astype(np.float32).astype(ml_dtypes.bfloat16)
    return high, low


def split(values):
    high = values.astype(BF16)
    low = (values - high.astype(F32)).astype(BF16)
    return high, low


def transform_tables():
    n = np.arange(M)
    angle = 2.0 * math.pi / M * ((n[:, None] * n[None, :]) % M)
    cos, sin = np.cos(angle), np.sin(angle)
    tab1 = np.stack([*split_np(cos), *split_np(sin)])
    def spread(t):
        t = t.reshape(M, R, CXL)
        return np.stack([t, t], axis=2).reshape(M, 2 * M)

    tab2 = np.stack(split_np(np.concatenate([spread(cos), -spread(sin)], axis=1)))
    t = np.arange(R)
    turn = 2.0 * math.pi / N * (t[:, None] * n[None, :])
    tw1 = np.stack([np.cos(turn), np.sin(turn)], axis=1).astype(np.float32).reshape(2 * R, M)
    scale = 1.0 / (N * N)
    tw2 = np.stack([np.cos(turn), np.sin(turn)], axis=1) * scale
    tw2 = tw2.reshape(R, 2, R, 1, CXL)
    tw2 = np.broadcast_to(tw2, (R, 2, R, 2, CXL)).astype(np.float32).reshape(R * 2 * R, 2 * CXL)

    def three(turns):
        high = turns.astype(ml_dtypes.bfloat16)
        mid = (turns - high.astype(np.float32)).astype(ml_dtypes.bfloat16)
        low = (turns - high.astype(np.float32) - mid.astype(np.float32)).astype(ml_dtypes.bfloat16)
        return np.concatenate([high, mid, low], axis=1)

    blob = np.zeros((BLOB, N), ml_dtypes.bfloat16)
    blob[:512] = tab2.reshape(512, N)
    blob[512:768] = tab1.transpose(1, 0, 2).reshape(M, N)
    blob[768:768 + 2 * R, :3 * M] = three(tw1)
    blob[784:784 + 2 * R * R, :6 * CXL] = three(tw2)
    return blob


def gauss_tables():
    alpha = (2.0 / (W * W)) * 16.0 ** (np.arange(NE) / (NE - 1))
    offs = np.arange(W) - W // 2
    shift = np.arange(SPAN) - SPAN // 2
    e = alpha[None, :, None, None] * (offs**2)[None, None, None, :]
    f = alpha[None, None, :, None] * ((offs[None, :] + shift[:, None]) ** 2)[:, None, None, :]
    grid = np.exp(-(e + f)).reshape(SPAN, ROWS, W).transpose(0, 2, 1)
    grid = np.concatenate([grid, np.zeros((SPAN, W, WIDE - ROWS))], axis=2)
    depth = np.zeros(WIDE)
    depth[:ROWS] = np.exp(-(alpha[:, None] + alpha[None, :]) * 0.25).reshape(-1) / W
    return np.concatenate([*split_np(grid), *split_np(grid * depth)], axis=2)


def butterfly(re, im):
    ar, br, cr, dr = re[0] + re[2], re[0] - re[2], re[1] + re[3], re[1] - re[3]
    ai, bi, ci, di = im[0] + im[2], im[0] - im[2], im[1] + im[3], im[1] - im[3]
    return (
        (ar + cr, ai + ci),
        (br - di, bi + dr),
        (ar - cr, ai - ci),
        (br + di, bi - dr),
    )


def transform_kernel(
    kpot, blob, pot, padded, tabs, tw1, tw2, z1h, z1l, fsend, grecv, z2h, z2l, yx,
    load_sem, send_sem, recv_sem, rim_send, rim_recv,
):
    spans = ((512, USED), (0, 512))
    loads = [
        pltpu.make_async_copy(blob.at[a:b], tabs.at[a:b], load_sem.at[i])
        for i, (a, b) in enumerate(spans)
    ]
    for load in loads:
        load.start()
    me = lax.axis_index("gx")
    count = 16
    barrier = pltpu.get_barrier_semaphore()
    for k in range(1, count):
        pl.semaphore_signal(
            barrier, inc=1, device_id={"gx": lax.rem(me + k, count)}, device_id_type=MESH
        )

    loads[0].wait()
    turns = tabs[768:784, :3 * M].astype(F32)
    tw1[...] = (turns[:, :M] + turns[:, M:2 * M] + turns[:, 2 * M:])[:2 * R]
    turns = tabs[784:816, :6 * CXL].astype(F32)
    tw2[...] = turns[:, :128] + turns[:, 128:256] + turns[:, 256:]
    for p in range(2):
        def rows_step(c, carry, p=p):
            row = pl.multiple_of(c * 16, 16)
            re = [kpot[0, p, pl.ds(row, 16), s * M:(s + 1) * M] for s in range(R)]
            im = [kpot[1, p, pl.ds(row, 16), s * M:(s + 1) * M] for s in range(R)]
            for t, (yr, yi) in enumerate(butterfly(re, im)):
                if t:
                    wr = tw1[2 * t:2 * t + 1, :]
                    wi = tw1[2 * t + 1:2 * t + 2, :]
                    yr, yi = yr * wr - yi * wi, yr * wi + yi * wr
                for c_at, part in enumerate((yr, yi)):
                    high, low = split(part)
                    at = pl.ds(pl.multiple_of(c_at * 128 + p * 64 + row, 16), 16)
                    z1h[t, at, :] = high
                    z1l[t, at, :] = low
            return carry
        lax.fori_loop(0, 4, rows_step, 0)

    for t in range(R):
        zh, zl = z1h[t], z1l[t]
        def tab1(at):
            return tabs[512:768, at * M:(at + 1) * M]
        def three(at):
            out = lax.dot_general(tab1(at), zh, NT, preferred_element_type=F32)
            out += lax.dot_general(tab1(at), zl, NT, preferred_element_type=F32)
            out += lax.dot_general(tab1(at + 1), zh, NT, preferred_element_type=F32)
            return out
        cz = three(0)
        sz = three(2)
        fre = cz[:, :128] - sz[:, 128:]
        fim = sz[:, :128] + cz[:, 128:]
        for d in range(count):
            fsend[d, 0, pl.ds(t, 16, stride=R), :] = fre[d * 16:(d + 1) * 16]
            fsend[d, 1, pl.ds(t, 16, stride=R), :] = fim[d * 16:(d + 1) * 16]

    pl.semaphore_wait(barrier, count - 1)
    copies = []
    for k in (8, 7, 9, 6, 10, 5, 11, 4, 12, 3, 13, 2, 14, 15, 1):
        other = lax.rem(me + k, count)
        copy = pltpu.make_async_remote_copy(
            src_ref=fsend.at[other],
            dst_ref=grecv.at[me],
            send_sem=send_sem.at[k],
            recv_sem=recv_sem.at[k],
            device_id={"gx": other},
            device_id_type=MESH,
        )
        copy.start()
        copies.append(copy)
    grecv[me] = fsend[me]
    loads[1].wait()
    for copy in copies:
        copy.wait()

    lane = lax.broadcasted_iota(jnp.int32, (16, 128), 1)
    for j in range(R):
        def cells_step(c, carry, j=j):
            row = pl.multiple_of(c * 16, 16)
            re = [grecv[R * s + j, 0, pl.ds(row, 16), :] for s in range(R)]
            im = [grecv[R * s + j, 1, pl.ds(row, 16), :] for s in range(R)]
            for t, (yr, yi) in enumerate(butterfly(re, im)):
                base = t * 2 * R + j
                wr = tw2[base:base + 1, :]
                if t:
                    wi = tw2[base + R:base + R + 1, :]
                    yr, yi = yr * wr - yi * wi, yr * wi + yi * wr
                else:
                    yr, yi = yr * wr, yi * wr
                for c_at, part in enumerate((yr, yi)):
                    for p in range(2):
                        mine = jnp.where((lane >= 64) == (p == 1), part, 0.0)
                        high, low = split(mine)
                        at = pl.ds(pl.multiple_of(t * 128 + p * 64 + row, 16), 16)
                        cols = slice((c_at * R + j) * 128, (c_at * R + j + 1) * 128)
                        z2h[at, cols] = high
                        z2l[at, cols] = low
            return carry
        lax.fori_loop(0, 4, cells_step, 0)

    for half in range(2):
        zh = z2h[half * 256:(half + 1) * 256, :]
        zl = z2l[half * 256:(half + 1) * 256, :]
        out = lax.dot_general(tabs[:M], zh, NT, preferred_element_type=F32)
        out += lax.dot_general(tabs[:M], zl, NT, preferred_element_type=F32)
        out += lax.dot_general(tabs[M:2 * M], zh, NT, preferred_element_type=F32)
        for i in range(2):
            yx[pl.ds(half * 2 + i, M, stride=R), :] = out[:, i * 128:(i + 1) * 128]
    for b in range(N // 128):
        tile = jnp.transpose(yx[b * 128:(b + 1) * 128, :])
        cols = slice(b * 128, (b + 1) * 128)
        pot[0, :, cols] = tile[:64]
        pot[1, :, cols] = tile[64:]
        total = tile[:64] + tile[64:]
        padded[b, 16:80, :] = total
        if b == 0:
            padded[N // 128, 16:80, :] = total

    left = lax.rem(me + count - 1, count)
    right = lax.rem(me + 1, count)
    to_left = pltpu.make_async_remote_copy(
        src_ref=padded.at[:, 16:32, :], dst_ref=padded.at[:, 80:96, :],
        send_sem=rim_send.at[0], recv_sem=rim_recv.at[0],
        device_id={"gx": left}, device_id_type=MESH,
    )
    to_right = pltpu.make_async_remote_copy(
        src_ref=padded.at[:, 64:80, :], dst_ref=padded.at[:, 0:16, :],
        send_sem=rim_send.at[1], recv_sem=rim_recv.at[1],
        device_id={"gx": right}, device_id_type=MESH,
    )
    to_left.start()
    to_right.start()
    to_left.wait()
    to_right.wait()


def pairs_kernel(
    cell_s, pair_s, padded, expo_t, pair_v, block_v, slot_v, gauss, message, rows
):
    lane = lax.broadcasted_iota(jnp.int32, (W, 128), 1)
    use_low = ((lane >> 5) & 1) == 1
    blank = jnp.zeros((W, 128), BF16)

    def two(g, carry):
        tabs, cells, seconds = [], [], []
        for q in range(2):
            i = pair_s[0, 2 * g + q]
            j = pair_s[1, 2 * g + q]
            cy, cx = cell_s[0, i], cell_s[1, i]
            dy = ((cy - cell_s[0, j] + N // 2) & (N - 1)) - N // 2
            dx = cx - cell_s[1, j]
            start = (cy - W // 2) & (N - 1)
            tile = start >> 7
            off = start & 127
            turn = (-off) & 127
            low_part = pltpu.roll(padded[tile, pl.ds(cx, W), :], turn, 1)
            high_part = pltpu.roll(padded[tile + 1, pl.ds(cx, W), :], turn, 1)
            window = jnp.where(lane < 128 - off, low_part, high_part)
            window = jnp.where(lane < W, window, 0.0)
            window = window + pltpu.roll(window, 32, 1)
            window = window + pltpu.roll(window, 64, 1)
            high, low = split(window)
            both = jnp.where(use_low, low, high)
            cells.append(
                jnp.concatenate([both, blank] if q == 0 else [blank, both], axis=1)
            )
            high, low = gauss[dy + SPAN // 2, :, :WIDE], gauss[dy + SPAN // 2, :, WIDE:2 * WIDE]
            tabs += [high, high, low, low]
            high, low = gauss[dx + SPAN // 2, :, 2 * WIDE:3 * WIDE], gauss[dx + SPAN // 2, :, 3 * WIDE:]
            seconds.append(high.astype(F32) + low.astype(F32))
        t = jnp.dot(
            jnp.concatenate(cells, axis=0), jnp.concatenate(tabs, axis=0),
            preferred_element_type=F32,
        )
        for q in range(2):
            done = jnp.sum(t[q * W:(q + 1) * W] * seconds[q], axis=0, keepdims=True)
            rows[pl.ds(2 * g + q, 1), :] = done
        return carry

    lax.fori_loop(0, 64, two, 0, unroll=16)
    message[0:128, :] = jnp.transpose(rows[:, 0:128])
    message[128:ROWS, :] = jnp.transpose(rows[:, 128:256])[:ROWS - 128]

    sub = lax.broadcasted_iota(jnp.int32, (128, 128), 0)
    exps = expo_t[...].astype(F32).astype(BF16)
    for side in range(2):
        hot = jnp.where(pair_v[side:side + 1, :] == sub, 1.0, 0.0).astype(BF16)
        at = ROWS + 64 * side
        message[at:at + 64, :] = jnp.dot(exps, hot, preferred_element_type=F32)
    hot = jnp.where(block_v[...] == sub, 1.0, 0.0).astype(BF16)
    slots = jnp.broadcast_to(slot_v[...].astype(F32), (8, 128)).astype(BF16)
    message[ROWS + 128:MSG, :] = jnp.dot(slots, hot, preferred_element_type=F32)


def reduce_kernel(
    message, out, theirs, bits, xsel, hits, ebuf, part0, part1, part2, near0, near1, near2,
    row0, row1, row2, far0, far1, far2,
    sm_sem, rm_sem, sb_sem, rb_sem, sc_sem, rc_sem,
):
    parts, nears, rows_of, fars = (
        (part0, part1, part2), (near0, near1, near2), (row0, row1, row2), (far0, far1, far2)
    )
    gx = lax.axis_index("gx")
    gy = lax.axis_index("gy")
    z, xh, core = gx // 4, lax.rem(gx // 2, 2), lax.rem(gx, 2)
    xl, y = gy // 4, lax.rem(gy, 4)
    x = xh * 2 + xl
    sibling = {"gx": z * 4 + xh * 2 + (1 - core), "gy": gy}

    def at(kz, ky, kx):
        to_x = lax.rem(x + kx, 4)
        to_gx = lax.rem(z + kz, 4) * 4 + (to_x // 2) * 2 + core
        return {"gx": to_gx, "gy": lax.rem(to_x, 2) * 4 + lax.rem(y + ky, 4)}

    axes = (("y", "z", "x"), ("z", "y", "x"), ("x", "z", "y"))
    place_of = {"z": z, "y": y, "x": x}

    def along(h, k0, k1, k2):
        step = dict(zip(axes[h], (k0, k1, k2)))
        return at(step["z"], step["y"], step["x"])

    barrier = pltpu.get_barrier_semaphore()
    partners = [sibling] + [
        at(kz, ky, kx)
        for kz in range(4) for ky in range(4) for kx in range(4)
        if 0 in (kz, ky, kx) and (kz, ky, kx) != (0, 0, 0)
    ]
    for device in partners:
        pl.semaphore_signal(barrier, inc=1, device_id=device, device_id_type=MESH)
    pl.semaphore_wait(barrier, len(partners))

    def send(src, dst, ssem, rsem, device):
        copy = pltpu.make_async_remote_copy(
            src_ref=src, dst_ref=dst, send_sem=ssem, recv_sem=rsem,
            device_id=device, device_id_type=MESH,
        )
        copy.start()
        return copy

    swap = send(message, theirs, sm_sem.at[0], rm_sem.at[0], sibling)

    sub = lax.broadcasted_iota(jnp.int32, (64, 128), 0)

    def prepare(o, source):
        slot = source[ROWS + 128:ROWS + 129, :].astype(jnp.int32)
        where = {
            "z": slot >> 5, "x": ((slot >> 4) & 1) * 2 + ((slot >> 2) & 1), "y": slot & 3
        }
        kept = ((slot >> 3) & 1) == core
        for h in range(3):
            a, b, c = (where[axis] for axis in axes[h])
            place = jnp.where(kept, a * 16 + b * 4 + c, 64)
            hit = jnp.where(place == sub, 1.0, 0.0).astype(BF16)
            hits[h, :, o * 256:o * 256 + 128] = hit
            hits[h, :, o * 256 + 128:o * 256 + 256] = hit

        exponent = source[ROWS:ROWS + 64, :].astype(jnp.int32)
        for b in range(4):
            bits[o, b] = jnp.where((exponent & (1 << b)) != 0, 1.0, 0.0)

        def choose_second(c, carry):
            rows = pl.ds(pl.multiple_of(c * 16, 16), 16)
            mine = source[pl.ds(pl.multiple_of(ROWS + 64 + c * 16, 16), 16), :]
            masks = [mine == float(f) for f in range(1, NE)]
            for e in range(NE):
                got = jnp.broadcast_to(source[e * NE:e * NE + 1, :], (16, 128))
                for f in range(1, NE):
                    got = jnp.where(masks[f - 1], source[e * NE + f:e * NE + f + 1, :], got)
                xsel[o, 0, e, rows, :], xsel[o, 1, e, rows, :] = split(got)
            return carry

        lax.fori_loop(0, 4, choose_second, 0)

    def choose(h, o):
        k0 = sum(KS[:h])
        for c in range(4):
            rows = slice(c * 16, c * 16 + 16)
            held = [[xsel[o, s, e, rows, :] for e in range(NE)] for s in range(2)]

            def choose_first(g, carry, c=c, held=held):
                masks = [
                    [
                        jnp.broadcast_to(bits[o, b, pl.ds(k0 + g * STEP + k, 1), :], (16, 128)).astype(BF16) > 0.5
                        for b in range(4)
                    ]
                    for k in range(STEP)
                ]
                done = []
                for b0, b1, b2, b3 in masks:
                    for s in range(2):
                        got = held[s]
                        got = [jnp.where(b0, got[e + 1], got[e]) for e in range(0, NE, 2)]
                        got = [jnp.where(b1, got[e + 1], got[e]) for e in range(0, NE // 2, 2)]
                        done.append(jnp.where(b3, got[2], jnp.where(b2, got[1], got[0])))
                for k in range(STEP):
                    at = pl.ds(pl.multiple_of((g * STEP + k) * 64 + c * 16, 16), 16)
                    for s in range(2):
                        col = o * 256 + s * 128
                        ebuf[h % 2, at, col:col + 128] = done[2 * k + s]
                return carry

            lax.fori_loop(0, KS[h] // STEP, choose_first, 0)

    prepare(0, message)
    choose(0, 0)
    choose(1, 0)
    swap.wait_recv()
    prepare(1, theirs)
    second = {}
    for h in range(3):
        if h == 2:
            choose(2, 0)
        choose(h, 1)
        got = lax.dot_general(
            hits[h], ebuf[h % 2, :KS[h] * 64, :], NT, preferred_element_type=F32
        )
        for a in range(4):
            parts[h][a] = got[a * 16:(a + 1) * 16]
        mine = place_of[axes[h][0]]
        for k in (2, 1, 3):
            second[h, k] = send(
                parts[h].at[lax.rem(mine + k, 4)], nears[h].at[k - 1],
                sb_sem.at[h, k], rb_sem.at[h, k], along(h, k, 0, 0),
            )
    third = {}
    for h in range(3):
        for k in (1, 3, 2):
            second[h, k].wait_recv()
        total = parts[h][place_of[axes[h][0]]] + nears[h][0] + nears[h][1] + nears[h][2]
        for c in range(KS[h] // 2):
            rows_of[h][:, c, :] = total[:, c * 128:(c + 1) * 128]
        b, c = (place_of[axis] for axis in axes[h][1:])
        for kb in (2, 1, 3, 0):
            for kc in (2, 1, 3, 0):
                if kb or kc:
                    to = lax.rem(b + kb, 4) * 4 + lax.rem(c + kc, 4)
                    at_k = kb * 4 + kc
                    third[h, at_k] = send(
                        rows_of[h].at[to], fars[h].at[at_k - 1],
                        sc_sem.at[h, at_k], rc_sem.at[h, at_k], along(h, 0, kb, kc),
                    )
    for h in range(3):
        b, c = (place_of[axis] for axis in axes[h][1:])
        done = rows_of[h][b * 4 + c]
        for at_k in range(1, 16):
            third[h, at_k].wait_recv()
        for at_k in range(1, 16):
            done = done + fars[h][at_k - 1]
        k0 = sum(KS[:h])
        out[0, pl.ds(k0, KS[h] // 2, stride=2), :] = done[:, :64]
        out[0, pl.ds(k0 + 1, KS[h] // 2, stride=2), :] = done[:, 64:]
    swap.wait_send()
    for group in (second, third):
        for copy in group.values():
            copy.wait_send()


def body(kpot, atom_cell, expo, pair_atoms, pair_block, block_slot):
    vmem = pl.BlockSpec(memory_space=pltpu.VMEM)
    smem = pl.BlockSpec(memory_space=pltpu.SMEM)
    dma = pltpu.SemaphoreType.DMA
    blob = jnp.asarray(transform_tables())
    gauss = jnp.asarray(gauss_tables())
    potential, padded = pl.pallas_call(
        transform_kernel,
        out_shape=(
            jax.ShapeDtypeStruct((2, CXL, N), F32),
            jax.ShapeDtypeStruct((N // 128 + 1, 96, 128), F32),
        ),
        in_specs=[vmem, pl.BlockSpec(memory_space=pl.ANY)],
        out_specs=(vmem, vmem),
        scratch_shapes=[
            pltpu.VMEM((USED, N), BF16),
            pltpu.VMEM((2 * R, M), F32),
            pltpu.VMEM((2 * R * R, 2 * CXL), F32),
            pltpu.VMEM((R, 256, M), BF16),
            pltpu.VMEM((R, 256, M), BF16),
            pltpu.VMEM((16, 2, CXL, 128), F32),
            pltpu.VMEM((16, 2, CXL, 128), F32),
            pltpu.VMEM((512, N), BF16),
            pltpu.VMEM((512, N), BF16),
            pltpu.VMEM((N, 128), F32),
            dma((2,)), dma((16,)), dma((16,)), dma((2,)), dma((2,)),
        ],
        compiler_params=pltpu.CompilerParams(
            collective_id=0, has_side_effects=True, vmem_limit_bytes=51 * 2**20
        ),
        name="transform",
    )(kpot, blob)
    cell_t, pair_t = atom_cell.T, pair_atoms.T
    message = pl.pallas_call(
        pairs_kernel,
        out_shape=jax.ShapeDtypeStruct((MSG, 128), F32),
        in_specs=[smem, smem] + [vmem] * 6,
        out_specs=vmem,
        scratch_shapes=[pltpu.VMEM((128, WIDE), F32)],
        compiler_params=pltpu.CompilerParams(vmem_limit_bytes=16 * 2**20),
        name="pairs",
    )(
        cell_t, pair_t, padded, expo.T, pair_t,
        pair_block.reshape(1, -1), block_slot.reshape(1, -1), gauss,
    )
    units = [k // 2 for k in KS]
    own = pl.pallas_call(
        reduce_kernel,
        out_shape=jax.ShapeDtypeStruct((1, 64, 64), F32),
        in_specs=[vmem],
        out_specs=vmem,
        scratch_shapes=[
            pltpu.VMEM((MSG, 128), F32),
            pltpu.VMEM((2, 4, 64, 128), F32),
            pltpu.VMEM((2, 2, NE, 64, 128), BF16),
            pltpu.VMEM((3, 64, 512), BF16),
            pltpu.VMEM((2, max(KS) * 64, 512), BF16),
        ]
        + [pltpu.VMEM((4, 16, u * 128), F32) for u in units]
        + [pltpu.VMEM((3, 16, u * 128), F32) for u in units]
        + [pltpu.VMEM((16, u, 128), F32) for u in units]
        + [pltpu.VMEM((15, u, 128), F32) for u in units]
        + [dma((1,)), dma((1,)), dma((3, 4)), dma((3, 4)), dma((3, 16)), dma((3, 16))],
        compiler_params=pltpu.CompilerParams(
            collective_id=1, has_side_effects=True, vmem_limit_bytes=24 * 2**20
        ),
        name="reduce",
    )(message)
    return jnp.transpose(potential, (0, 2, 1)), own


def solution(mesh):
    return jax.shard_map(
        body,
        mesh=mesh,
        in_specs=(
            P(None, "gy", "gx", None),
            P(("gx", "gy"), None),
            P(("gx", "gy"), None),
            P(("gx", "gy"), None),
            P(("gx", "gy")),
            P(),
        ),
        out_specs=(P("gy", None, "gx"), P(("gx", "gy"), None, None)),
        check_vma=False,
    )
```

```python
import math

import jax
import jax.numpy as jnp
import ml_dtypes
import numpy as np
from jax import lax
from jax.experimental import pallas as pl
from jax.experimental.pallas import tpu as pltpu
from jax.sharding import PartitionSpec as P

W = 32
NE = 12
ROWS = NE * NE
WIDE = 256
SPAN = 33
N = 1024
R = 4
M = N // R
CXL = 64
KS = (24, 24, 16)
STEP = 8
MSG = 280
SENDS = (10, 11, 8, 9, 6, 7, 4, 5, 14, 15, 12, 13, 2, 3, 1)
LOOP_X = False
GROUP = 16
BLOB = 4096
USED = 816
MESH = pl.DeviceIdType.MESH
NT = (((1,), (1,)), ((), ()))
F32 = jnp.float32
BF16 = jnp.bfloat16


def split_np(values):
    high = values.astype(np.float32).astype(ml_dtypes.bfloat16)
    low = (values - high.astype(np.float64)).astype(np.float32).astype(ml_dtypes.bfloat16)
    return high, low


def split(values):
    high = values.astype(BF16)
    low = (values - high.astype(F32)).astype(BF16)
    return high, low


def transform_tables():
    n = np.arange(M)
    angle = 2.0 * math.pi / M * ((n[:, None] * n[None, :]) % M)
    cos, sin = np.cos(angle), np.sin(angle)
    tab1 = np.stack([*split_np(cos), *split_np(sin)])
    def spread(t):
        t = t.reshape(M, R, CXL)
        return np.stack([t, t], axis=2).reshape(M, 2 * M)

    tab2 = np.stack(split_np(np.concatenate([spread(cos), -spread(sin)], axis=1)))
    t = np.arange(R)
    turn = 2.0 * math.pi / N * (t[:, None] * n[None, :])
    tw1 = np.stack([np.cos(turn), np.sin(turn)], axis=1).astype(np.float32).reshape(2 * R, M)
    scale = 1.0 / (N * N)
    tw2 = np.stack([np.cos(turn), np.sin(turn)], axis=1) * scale
    tw2 = tw2.reshape(R, 2, R, 1, CXL)
    tw2 = np.broadcast_to(tw2, (R, 2, R, 2, CXL)).astype(np.float32).reshape(R * 2 * R, 2 * CXL)

    def three(turns):
        high = turns.astype(ml_dtypes.bfloat16)
        mid = (turns - high.astype(np.float32)).astype(ml_dtypes.bfloat16)
        low = (turns - high.astype(np.float32) - mid.astype(np.float32)).astype(ml_dtypes.bfloat16)
        return np.concatenate([high, mid, low], axis=1)

    blob = np.zeros((BLOB, N), ml_dtypes.bfloat16)
    blob[:512] = tab2.reshape(512, N)
    blob[512:768] = tab1.transpose(1, 0, 2).reshape(M, N)
    blob[768:768 + 2 * R, :3 * M] = three(tw1)
    blob[784:784 + 2 * R * R, :6 * CXL] = three(tw2)
    return blob


def gauss_tables():
    alpha = (2.0 / (W * W)) * 16.0 ** (np.arange(NE) / (NE - 1))
    offs = np.arange(W) - W // 2
    shift = np.arange(SPAN) - SPAN // 2
    e = alpha[None, :, None, None] * (offs**2)[None, None, None, :]
    f = alpha[None, None, :, None] * ((offs[None, :] + shift[:, None]) ** 2)[:, None, None, :]
    grid = np.exp(-(e + f)).reshape(SPAN, ROWS, W).transpose(0, 2, 1)
    grid = np.concatenate([grid, np.zeros((SPAN, W, WIDE - ROWS))], axis=2)
    depth = np.zeros(WIDE)
    depth[:ROWS] = np.exp(-(alpha[:, None] + alpha[None, :]) * 0.25).reshape(-1) / W
    return np.concatenate([*split_np(grid), *split_np(grid * depth)], axis=2)


def butterfly(re, im):
    ar, br, cr, dr = re[0] + re[2], re[0] - re[2], re[1] + re[3], re[1] - re[3]
    ai, bi, ci, di = im[0] + im[2], im[0] - im[2], im[1] + im[3], im[1] - im[3]
    return (
        (ar + cr, ai + ci),
        (br - di, bi + dr),
        (ar - cr, ai - ci),
        (br + di, bi - dr),
    )


def transform_kernel(
    kpot_any, blob, pot, padded, kpot, tabs, tw1, tw2, z1h, z1l, fsend, grecv, z2h, z2l, yx,
    load_sem, send_sem, recv_sem, rim_send, rim_recv,
):
    moves = (
        (kpot_any.at[:, 0], kpot.at[:, 0]),
        (blob.at[768:USED], tabs.at[768:USED]),
        (kpot_any.at[:, 1], kpot.at[:, 1]),
        (blob.at[512:768], tabs.at[512:768]),
        (blob.at[0:512], tabs.at[0:512]),
    )
    loads = [
        pltpu.make_async_copy(source, target, load_sem.at[i])
        for i, (source, target) in enumerate(moves)
    ]
    for load in loads:
        load.start()
    me = lax.axis_index("gx")
    count = 16
    barrier = pltpu.get_barrier_semaphore()
    for k in range(1, count):
        pl.semaphore_signal(
            barrier, inc=1, device_id={"gx": lax.rem(me + k, count)}, device_id_type=MESH
        )

    loads[1].wait()
    turns = tabs[768:784, :3 * M].astype(F32)
    tw1[...] = (turns[:, :M] + turns[:, M:2 * M] + turns[:, 2 * M:])[:2 * R]
    turns = tabs[784:816, :6 * CXL].astype(F32)
    tw2[...] = turns[:, :128] + turns[:, 128:256] + turns[:, 256:]
    for p in range(2):
        loads[2 * p].wait()

        def rows_step(c, carry, p=p):
            row = pl.multiple_of(c * 16, 16)
            re = [kpot[0, p, pl.ds(row, 16), s * M:(s + 1) * M] for s in range(R)]
            im = [kpot[1, p, pl.ds(row, 16), s * M:(s + 1) * M] for s in range(R)]
            for t, (yr, yi) in enumerate(butterfly(re, im)):
                if t:
                    wr = tw1[2 * t:2 * t + 1, :]
                    wi = tw1[2 * t + 1:2 * t + 2, :]
                    yr, yi = yr * wr - yi * wi, yr * wi + yi * wr
                for c_at, part in enumerate((yr, yi)):
                    high, low = split(part)
                    at = pl.ds(pl.multiple_of(c_at * 128 + p * 64 + row, 16), 16)
                    z1h[t, at, :] = high
                    z1l[t, at, :] = low
            return carry
        lax.fori_loop(0, 4, rows_step, 0)

    loads[3].wait()

    def stage_x(t, carry):
        zh, zl = z1h[t], z1l[t]

        def three(at):
            table = tabs[512:768, at * M:(at + 1) * M]
            out = lax.dot_general(table, zh, NT, preferred_element_type=F32)
            out += lax.dot_general(table, zl, NT, preferred_element_type=F32)
            table = tabs[512:768, (at + 1) * M:(at + 2) * M]
            out += lax.dot_general(table, zh, NT, preferred_element_type=F32)
            return out

        cz = three(0)
        sz = three(2)
        fre = cz[:, :128] - sz[:, 128:]
        fim = sz[:, :128] + cz[:, 128:]
        for d in range(count):
            fsend[d, 0, pl.ds(t, 16, stride=R), :] = fre[d * 16:(d + 1) * 16]
            fsend[d, 1, pl.ds(t, 16, stride=R), :] = fim[d * 16:(d + 1) * 16]
        return carry

    if LOOP_X:
        lax.fori_loop(0, R, stage_x, 0)
    else:
        for t in range(R):
            stage_x(t, 0)

    pl.semaphore_wait(barrier, count - 1)
    copies = []
    for k in SENDS:
        other = lax.rem(me // 4 + k // 4, 4) * 4 + jnp.bitwise_xor(lax.rem(me, 4), k % 4)
        copy = pltpu.make_async_remote_copy(
            src_ref=fsend.at[other],
            dst_ref=grecv.at[me],
            send_sem=send_sem.at[k],
            recv_sem=recv_sem.at[k],
            device_id={"gx": other},
            device_id_type=MESH,
        )
        copy.start()
        copies.append(copy)
    grecv[me] = fsend[me]
    loads[4].wait()
    for copy in copies:
        copy.wait()

    lane = lax.broadcasted_iota(jnp.int32, (16, 128), 1)
    for j in range(R):
        def cells_step(c, carry, j=j):
            row = pl.multiple_of(c * 16, 16)
            re = [grecv[R * s + j, 0, pl.ds(row, 16), :] for s in range(R)]
            im = [grecv[R * s + j, 1, pl.ds(row, 16), :] for s in range(R)]
            for t, (yr, yi) in enumerate(butterfly(re, im)):
                base = t * 2 * R + j
                wr = tw2[base:base + 1, :]
                if t:
                    wi = tw2[base + R:base + R + 1, :]
                    yr, yi = yr * wr - yi * wi, yr * wi + yi * wr
                else:
                    yr, yi = yr * wr, yi * wr
                for c_at, part in enumerate((yr, yi)):
                    for p in range(2):
                        mine = jnp.where((lane >= 64) == (p == 1), part, 0.0)
                        high, low = split(mine)
                        at = pl.ds(pl.multiple_of(t * 128 + p * 64 + row, 16), 16)
                        cols = slice((c_at * R + j) * 128, (c_at * R + j + 1) * 128)
                        z2h[at, cols] = high
                        z2l[at, cols] = low
            return carry
        lax.fori_loop(0, 4, cells_step, 0)

    for half in range(2):
        zh = z2h[half * 256:(half + 1) * 256, :]
        zl = z2l[half * 256:(half + 1) * 256, :]
        out = lax.dot_general(tabs[:M], zh, NT, preferred_element_type=F32)
        out += lax.dot_general(tabs[:M], zl, NT, preferred_element_type=F32)
        out += lax.dot_general(tabs[M:2 * M], zh, NT, preferred_element_type=F32)
        for i in range(2):
            yx[pl.ds(half * 2 + i, M, stride=R), :] = out[:, i * 128:(i + 1) * 128]
    for b in range(N // 128):
        tile = jnp.transpose(yx[b * 128:(b + 1) * 128, :])
        cols = slice(b * 128, (b + 1) * 128)
        pot[0, :, cols] = tile[:64]
        pot[1, :, cols] = tile[64:]
        total = tile[:64] + tile[64:]
        padded[b, 16:80, :] = total
        if b == 0:
            padded[N // 128, 16:80, :] = total

    left = lax.rem(me + count - 1, count)
    right = lax.rem(me + 1, count)
    to_left = pltpu.make_async_remote_copy(
        src_ref=padded.at[:, 16:32, :], dst_ref=padded.at[:, 80:96, :],
        send_sem=rim_send.at[0], recv_sem=rim_recv.at[0],
        device_id={"gx": left}, device_id_type=MESH,
    )
    to_right = pltpu.make_async_remote_copy(
        src_ref=padded.at[:, 64:80, :], dst_ref=padded.at[:, 0:16, :],
        send_sem=rim_send.at[1], recv_sem=rim_recv.at[1],
        device_id={"gx": right}, device_id_type=MESH,
    )
    to_left.start()
    to_right.start()
    to_left.wait()
    to_right.wait()


def pairs_kernel(
    cell_s, pair_s, padded, expo_t, pair_v, block_v, slot_v, gauss, pot, message, pot_out, rows, pot_sem
):
    store = pltpu.make_async_copy(pot, pot_out, pot_sem)
    store.start()
    lane = lax.broadcasted_iota(jnp.int32, (W, 128), 1)
    use_low = ((lane >> 5) & 1) == 1
    blank = jnp.zeros((W, 128), BF16)

    def several(step, carry):
        operands, scales = [], []
        for n in range(GROUP):
            tabs, cells = [], []
            for q in range(2):
                p = (step * GROUP + n) * 2 + q
                i = pair_s[0, p]
                j = pair_s[1, p]
                cy, cx = cell_s[0, i], cell_s[1, i]
                dy = ((cy - cell_s[0, j] + N // 2) & (N - 1)) - N // 2
                dx = cx - cell_s[1, j]
                start = (cy - W // 2) & (N - 1)
                tile = start >> 7
                off = start & 127
                turn = (-off) & 127
                low_part = pltpu.roll(padded[tile, pl.ds(cx, W), :], turn, 1)
                high_part = pltpu.roll(padded[tile + 1, pl.ds(cx, W), :], turn, 1)
                window = jnp.where(lane < 128 - off, low_part, high_part)
                window = jnp.where(lane < W, window, 0.0)
                window = window + pltpu.roll(window, 32, 1)
                window = window + pltpu.roll(window, 64, 1)
                high, low = split(window)
                both = jnp.where(use_low, low, high)
                cells.append(
                    jnp.concatenate([both, blank] if q == 0 else [blank, both], axis=1)
                )
                high, low = gauss[dy + SPAN // 2, :, :WIDE], gauss[dy + SPAN // 2, :, WIDE:2 * WIDE]
                tabs += [high, high, low, low]
                scales.append(dx + SPAN // 2)
            operands.append((jnp.concatenate(cells, axis=0), jnp.concatenate(tabs, axis=0)))
        done = []
        for n in range(GROUP):
            t = jnp.dot(*operands[n], preferred_element_type=F32)
            for q in range(2):
                at = scales[2 * n + q]
                high, low = gauss[at, :, 2 * WIDE:3 * WIDE], gauss[at, :, 3 * WIDE:]
                scaled = t[q * W:(q + 1) * W] * (high.astype(F32) + low.astype(F32))
                done.append(jnp.sum(scaled, axis=0, keepdims=True))
        at = pl.ds(pl.multiple_of(step * GROUP * 2, GROUP * 2), GROUP * 2)
        rows[at, :] = jnp.concatenate(done, axis=0)
        return carry

    lax.fori_loop(0, 64 // GROUP, several, 0)
    message[0:128, :] = jnp.transpose(rows[:, 0:128])
    message[128:ROWS, :] = jnp.transpose(rows[:, 128:256])[:ROWS - 128]

    sub = lax.broadcasted_iota(jnp.int32, (128, 128), 0)
    exps = expo_t[...].astype(F32).astype(BF16)
    for side in range(2):
        hot = jnp.where(pair_v[side:side + 1, :] == sub, 1.0, 0.0).astype(BF16)
        at = ROWS + 64 * side
        message[at:at + 64, :] = jnp.dot(exps, hot, preferred_element_type=F32)
    hot = jnp.where(block_v[...] == sub, 1.0, 0.0).astype(BF16)
    slots = jnp.broadcast_to(slot_v[...].astype(F32), (8, 128)).astype(BF16)
    message[ROWS + 128:MSG, :] = jnp.dot(slots, hot, preferred_element_type=F32)
    store.wait()


def reduce_kernel(
    message, out, theirs, bits, xsel, hits, ebuf, part0, part1, part2, near0, near1, near2,
    row0, row1, row2, far0, far1, far2,
    sm_sem, rm_sem, sb_sem, rb_sem, sc_sem, rc_sem,
):
    parts, nears, rows_of, fars = (
        (part0, part1, part2), (near0, near1, near2), (row0, row1, row2), (far0, far1, far2)
    )
    gx = lax.axis_index("gx")
    gy = lax.axis_index("gy")
    z, xh, core = gx // 4, lax.rem(gx // 2, 2), lax.rem(gx, 2)
    xl, y = gy // 4, lax.rem(gy, 4)
    x = xh * 2 + xl
    sibling = {"gx": z * 4 + xh * 2 + (1 - core), "gy": gy}

    def at(kz, ky, kx):
        to_x = lax.rem(x + kx, 4)
        to_gx = lax.rem(z + kz, 4) * 4 + (to_x // 2) * 2 + core
        return {"gx": to_gx, "gy": lax.rem(to_x, 2) * 4 + lax.rem(y + ky, 4)}

    axes = (("y", "z", "x"), ("z", "y", "x"), ("x", "z", "y"))
    place_of = {"z": z, "y": y, "x": x}

    def along(h, k0, k1, k2):
        step = dict(zip(axes[h], (k0, k1, k2)))
        return at(step["z"], step["y"], step["x"])

    barrier = pltpu.get_barrier_semaphore()
    partners = [sibling] + [
        at(kz, ky, kx)
        for kz in range(4) for ky in range(4) for kx in range(4)
        if 0 in (kz, ky, kx) and (kz, ky, kx) != (0, 0, 0)
    ]
    for device in partners:
        pl.semaphore_signal(barrier, inc=1, device_id=device, device_id_type=MESH)
    pl.semaphore_wait(barrier, len(partners))

    def send(src, dst, ssem, rsem, device):
        copy = pltpu.make_async_remote_copy(
            src_ref=src, dst_ref=dst, send_sem=ssem, recv_sem=rsem,
            device_id=device, device_id_type=MESH,
        )
        copy.start()
        return copy

    swap = send(message, theirs, sm_sem.at[0], rm_sem.at[0], sibling)

    sub = lax.broadcasted_iota(jnp.int32, (64, 128), 0)

    def prepare(o, source):
        slot = source[ROWS + 128:ROWS + 129, :].astype(jnp.int32)
        where = {
            "z": slot >> 5, "x": ((slot >> 4) & 1) * 2 + ((slot >> 2) & 1), "y": slot & 3
        }
        kept = ((slot >> 3) & 1) == core
        for h in range(3):
            a, b, c = (where[axis] for axis in axes[h])
            place = jnp.where(kept, a * 16 + b * 4 + c, 64)
            hit = jnp.where(place == sub, 1.0, 0.0).astype(BF16)
            hits[h, :, o * 256:o * 256 + 128] = hit
            hits[h, :, o * 256 + 128:o * 256 + 256] = hit

        exponent = source[ROWS:ROWS + 64, :].astype(jnp.int32)
        for b in range(4):
            bits[o, b] = jnp.where((exponent & (1 << b)) != 0, 1.0, 0.0)

        def choose_second(c, carry):
            rows = pl.ds(pl.multiple_of(c * 16, 16), 16)
            mine = source[pl.ds(pl.multiple_of(ROWS + 64 + c * 16, 16), 16), :]
            masks = [mine == float(f) for f in range(1, NE)]
            for e in range(NE):
                got = jnp.broadcast_to(source[e * NE:e * NE + 1, :], (16, 128))
                for f in range(1, NE):
                    got = jnp.where(masks[f - 1], source[e * NE + f:e * NE + f + 1, :], got)
                xsel[o, 0, e, rows, :], xsel[o, 1, e, rows, :] = split(got)
            return carry

        lax.fori_loop(0, 4, choose_second, 0)

    def choose(o, start, steps):
        def rows_step(c, carry):
            rows = pl.ds(pl.multiple_of(c * 16, 16), 16)
            held = [[xsel[o, s, e, rows, :] for e in range(NE)] for s in range(2)]

            def choose_first(g, carry):
                first = start + g * STEP
                masks = [
                    [
                        jnp.broadcast_to(bits[o, b, pl.ds(first + k, 1), :], (16, 128)).astype(BF16) > 0.5
                        for b in range(4)
                    ]
                    for k in range(STEP)
                ]
                done = []
                for b0, b1, b2, b3 in masks:
                    for s in range(2):
                        got = held[s]
                        got = [jnp.where(b0, got[e + 1], got[e]) for e in range(0, NE, 2)]
                        got = [jnp.where(b1, got[e + 1], got[e]) for e in range(0, NE // 2, 2)]
                        done.append(jnp.where(b3, got[2], jnp.where(b2, got[1], got[0])))
                for k in range(STEP):
                    at = pl.ds(pl.multiple_of((first + k) * 64 + c * 16, 16), 16)
                    for s in range(2):
                        col = o * 256 + s * 128
                        ebuf[at, col:col + 128] = done[2 * k + s]
                return carry

            lax.fori_loop(0, steps, choose_first, 0)
            return carry

        lax.fori_loop(0, 4, rows_step, 0)

    prepare(0, message)
    choose(0, 0, 64 // STEP)
    swap.wait_recv()
    prepare(1, theirs)
    second = {}
    for h in range(3):
        k0 = sum(KS[:h])
        choose(1, k0, KS[h] // STEP)
        got = lax.dot_general(
            hits[h], ebuf[k0 * 64:(k0 + KS[h]) * 64, :], NT, preferred_element_type=F32
        )
        for a in range(4):
            parts[h][a] = got[a * 16:(a + 1) * 16]
        mine = place_of[axes[h][0]]
        for k in (2, 1, 3):
            second[h, k] = send(
                parts[h].at[lax.rem(mine + k, 4)], nears[h].at[k - 1],
                sb_sem.at[h, k], rb_sem.at[h, k], along(h, k, 0, 0),
            )
    third = {}
    for h in range(3):
        for k in (1, 3, 2):
            second[h, k].wait_recv()
        total = parts[h][place_of[axes[h][0]]] + nears[h][0] + nears[h][1] + nears[h][2]
        for c in range(KS[h] // 2):
            rows_of[h][:, c, :] = total[:, c * 128:(c + 1) * 128]
        b, c = (place_of[axis] for axis in axes[h][1:])
        for kb in (2, 1, 3, 0):
            for kc in (2, 1, 3, 0):
                if kb or kc:
                    to = lax.rem(b + kb, 4) * 4 + lax.rem(c + kc, 4)
                    at_k = kb * 4 + kc
                    third[h, at_k] = send(
                        rows_of[h].at[to], fars[h].at[at_k - 1],
                        sc_sem.at[h, at_k], rc_sem.at[h, at_k], along(h, 0, kb, kc),
                    )
    for h in range(3):
        b, c = (place_of[axis] for axis in axes[h][1:])
        done = rows_of[h][b * 4 + c]
        for at_k in range(1, 16):
            third[h, at_k].wait_recv()
        for at_k in range(1, 16):
            done = done + fars[h][at_k - 1]
        k0 = sum(KS[:h])
        out[0, pl.ds(k0, KS[h] // 2, stride=2), :] = done[:, :64]
        out[0, pl.ds(k0 + 1, KS[h] // 2, stride=2), :] = done[:, 64:]
    swap.wait_send()
    for group in (second, third):
        for copy in group.values():
            copy.wait_send()


def body(kpot, atom_cell, expo, pair_atoms, pair_block, block_slot):
    vmem = pl.BlockSpec(memory_space=pltpu.VMEM)
    smem = pl.BlockSpec(memory_space=pltpu.SMEM)
    dma = pltpu.SemaphoreType.DMA
    blob = jnp.asarray(transform_tables())
    gauss = jnp.asarray(gauss_tables())
    potential, padded = pl.pallas_call(
        transform_kernel,
        out_shape=(
            jax.ShapeDtypeStruct((2, CXL, N), F32),
            jax.ShapeDtypeStruct((N // 128 + 1, 96, 128), F32),
        ),
        in_specs=[pl.BlockSpec(memory_space=pl.ANY)] * 2,
        out_specs=(vmem, vmem),
        scratch_shapes=[
            pltpu.VMEM(kpot.shape, F32),
            pltpu.VMEM((USED, N), BF16),
            pltpu.VMEM((2 * R, M), F32),
            pltpu.VMEM((2 * R * R, 2 * CXL), F32),
            pltpu.VMEM((R, 256, M), BF16),
            pltpu.VMEM((R, 256, M), BF16),
            pltpu.VMEM((16, 2, CXL, 128), F32),
            pltpu.VMEM((16, 2, CXL, 128), F32),
            pltpu.VMEM((512, N), BF16),
            pltpu.VMEM((512, N), BF16),
            pltpu.VMEM((N, 128), F32),
            dma((5,)), dma((16,)), dma((16,)), dma((2,)), dma((2,)),
        ],
        compiler_params=pltpu.CompilerParams(
            collective_id=0, has_side_effects=True, vmem_limit_bytes=211 * 2**18
        ),
        name="transform",
    )(kpot, blob)
    cell_t, pair_t = atom_cell.T, pair_atoms.T
    message, potential = pl.pallas_call(
        pairs_kernel,
        out_shape=(
            jax.ShapeDtypeStruct((MSG, 128), F32), jax.ShapeDtypeStruct(potential.shape, F32)
        ),
        in_specs=[smem, smem] + [vmem] * 6 + [pl.BlockSpec(memory_space=pl.ANY)],
        out_specs=(vmem, pl.BlockSpec(memory_space=pl.ANY)),
        scratch_shapes=[pltpu.VMEM((128, WIDE), F32), dma],
        compiler_params=pltpu.CompilerParams(vmem_limit_bytes=16 * 2**20),
        name="pairs",
    )(
        cell_t, pair_t, padded, expo.T, pair_t,
        pair_block.reshape(1, -1), block_slot.reshape(1, -1), gauss, potential,
    )
    units = [k // 2 for k in KS]
    own = pl.pallas_call(
        reduce_kernel,
        out_shape=jax.ShapeDtypeStruct((1, 64, 64), F32),
        in_specs=[vmem],
        out_specs=vmem,
        scratch_shapes=[
            pltpu.VMEM((MSG, 128), F32),
            pltpu.VMEM((2, 4, 64, 128), F32),
            pltpu.VMEM((2, 2, NE, 64, 128), BF16),
            pltpu.VMEM((3, 64, 512), BF16),
            pltpu.VMEM((4096, 512), BF16),
        ]
        + [pltpu.VMEM((4, 16, u * 128), F32) for u in units]
        + [pltpu.VMEM((3, 16, u * 128), F32) for u in units]
        + [pltpu.VMEM((16, u, 128), F32) for u in units]
        + [pltpu.VMEM((15, u, 128), F32) for u in units]
        + [dma((1,)), dma((1,)), dma((3, 4)), dma((3, 4)), dma((3, 16)), dma((3, 16))],
        compiler_params=pltpu.CompilerParams(
            collective_id=1, has_side_effects=True, vmem_limit_bytes=24 * 2**20
        ),
        name="reduce",
    )(message)
    return jnp.transpose(potential, (0, 2, 1)), own


def solution(mesh):
    return jax.shard_map(
        body,
        mesh=mesh,
        in_specs=(
            P(None, "gy", "gx", None),
            P(("gx", "gy"), None),
            P(("gx", "gy"), None),
            P(("gx", "gy"), None),
            P(("gx", "gy")),
            P(),
        ),
        out_specs=(P("gy", None, "gx"), P(("gx", "gy"), None, None)),
        check_vma=False,
    )
```

```python
import math

import jax
import jax.numpy as jnp
import ml_dtypes
import numpy as np
from jax import lax
from jax.experimental import pallas as pl
from jax.experimental.pallas import tpu as pltpu
from jax.sharding import PartitionSpec as P

W = 32
NE = 12
ROWS = NE * NE
WIDE = 256
SPAN = 33
N = 1024
R = 4
M = N // R
CXL = 64
KS = (24, 22, 18)
SIZES = (8, 11, 9)
STEP = 8
MSG = 280
SENDS = (10, 11, 8, 9, 6, 7, 4, 5, 14, 15, 12, 13, 2, 3, 1)
LOOP_X = False
GROUP = 16
BLOB = 4096
USED = 816
MESH = pl.DeviceIdType.MESH
NT = (((1,), (1,)), ((), ()))
F32 = jnp.float32
BF16 = jnp.bfloat16


def split_np(values):
    high = values.astype(np.float32).astype(ml_dtypes.bfloat16)
    low = (values - high.astype(np.float64)).astype(np.float32).astype(ml_dtypes.bfloat16)
    return high, low


def split(values):
    high = values.astype(BF16)
    low = (values - high.astype(F32)).astype(BF16)
    return high, low


def transform_tables():
    n = np.arange(M)
    angle = 2.0 * math.pi / M * ((n[:, None] * n[None, :]) % M)
    cos, sin = np.cos(angle), np.sin(angle)
    tab1 = np.stack([*split_np(cos), *split_np(sin)])
    def spread(t):
        t = t.reshape(M, R, CXL)
        return np.stack([t, t], axis=2).reshape(M, 2 * M)

    tab2 = np.stack(split_np(np.concatenate([spread(cos), -spread(sin)], axis=1)))
    t = np.arange(R)
    turn = 2.0 * math.pi / N * (t[:, None] * n[None, :])
    tw1 = np.stack([np.cos(turn), np.sin(turn)], axis=1).astype(np.float32).reshape(2 * R, M)
    scale = 1.0 / (N * N)
    tw2 = np.stack([np.cos(turn), np.sin(turn)], axis=1) * scale
    tw2 = tw2.reshape(R, 2, R, 1, CXL)
    tw2 = np.broadcast_to(tw2, (R, 2, R, 2, CXL)).astype(np.float32).reshape(R * 2 * R, 2 * CXL)

    def three(turns):
        high = turns.astype(ml_dtypes.bfloat16)
        mid = (turns - high.astype(np.float32)).astype(ml_dtypes.bfloat16)
        low = (turns - high.astype(np.float32) - mid.astype(np.float32)).astype(ml_dtypes.bfloat16)
        return np.concatenate([high, mid, low], axis=1)

    blob = np.zeros((BLOB, N), ml_dtypes.bfloat16)
    blob[:512] = tab2.reshape(512, N)
    blob[512:768] = tab1.transpose(1, 0, 2).reshape(M, N)
    blob[768:768 + 2 * R, :3 * M] = three(tw1)
    blob[784:784 + 2 * R * R, :6 * CXL] = three(tw2)
    return blob


def gauss_tables():
    alpha = (2.0 / (W * W)) * 16.0 ** (np.arange(NE) / (NE - 1))
    offs = np.arange(W) - W // 2
    shift = np.arange(SPAN) - SPAN // 2
    e = alpha[None, :, None, None] * (offs**2)[None, None, None, :]
    f = alpha[None, None, :, None] * ((offs[None, :] + shift[:, None]) ** 2)[:, None, None, :]
    grid = np.exp(-(e + f)).reshape(SPAN, ROWS, W).transpose(0, 2, 1)
    grid = np.concatenate([grid, np.zeros((SPAN, W, WIDE - ROWS))], axis=2)
    depth = np.zeros(WIDE)
    depth[:ROWS] = np.exp(-(alpha[:, None] + alpha[None, :]) * 0.25).reshape(-1) / W
    return np.concatenate([*split_np(grid), *split_np(grid * depth)], axis=2)


def butterfly(re, im):
    ar, br, cr, dr = re[0] + re[2], re[0] - re[2], re[1] + re[3], re[1] - re[3]
    ai, bi, ci, di = im[0] + im[2], im[0] - im[2], im[1] + im[3], im[1] - im[3]
    return (
        (ar + cr, ai + ci),
        (br - di, bi + dr),
        (ar - cr, ai - ci),
        (br + di, bi - dr),
    )


def transform_kernel(
    kpot_any, blob, pot, padded, kpot, tabs, tw1, tw2, z1h, z1l, fsend, grecv, z2h, z2l, yx,
    load_sem, send_sem, recv_sem, rim_send, rim_recv,
):
    moves = (
        (kpot_any.at[:, 0], kpot.at[:, 0]),
        (blob.at[768:USED], tabs.at[768:USED]),
        (kpot_any.at[:, 1], kpot.at[:, 1]),
        (blob.at[512:768], tabs.at[512:768]),
        (blob.at[0:512], tabs.at[0:512]),
    )
    loads = [
        pltpu.make_async_copy(source, target, load_sem.at[i])
        for i, (source, target) in enumerate(moves)
    ]
    for load in loads:
        load.start()
    me = lax.axis_index("gx")
    count = 16
    barrier = pltpu.get_barrier_semaphore()
    for k in range(1, count):
        pl.semaphore_signal(
            barrier, inc=1, device_id={"gx": lax.rem(me + k, count)}, device_id_type=MESH
        )

    loads[1].wait()
    turns = tabs[768:784, :3 * M].astype(F32)
    tw1[...] = (turns[:, :M] + turns[:, M:2 * M] + turns[:, 2 * M:])[:2 * R]
    turns = tabs[784:816, :6 * CXL].astype(F32)
    tw2[...] = turns[:, :128] + turns[:, 128:256] + turns[:, 256:]
    for p in range(2):
        loads[2 * p].wait()

        def rows_step(c, carry, p=p):
            row = pl.multiple_of(c * 16, 16)
            re = [kpot[0, p, pl.ds(row, 16), s * M:(s + 1) * M] for s in range(R)]
            im = [kpot[1, p, pl.ds(row, 16), s * M:(s + 1) * M] for s in range(R)]
            for t, (yr, yi) in enumerate(butterfly(re, im)):
                if t:
                    wr = tw1[2 * t:2 * t + 1, :]
                    wi = tw1[2 * t + 1:2 * t + 2, :]
                    yr, yi = yr * wr - yi * wi, yr * wi + yi * wr
                for c_at, part in enumerate((yr, yi)):
                    high, low = split(part)
                    at = pl.ds(pl.multiple_of(c_at * 128 + p * 64 + row, 16), 16)
                    z1h[t, at, :] = high
                    z1l[t, at, :] = low
            return carry
        lax.fori_loop(0, 4, rows_step, 0)

    loads[3].wait()

    def stage_x(t, carry):
        zh, zl = z1h[t], z1l[t]

        def three(at):
            table = tabs[512:768, at * M:(at + 1) * M]
            out = lax.dot_general(table, zh, NT, preferred_element_type=F32)
            out += lax.dot_general(table, zl, NT, preferred_element_type=F32)
            table = tabs[512:768, (at + 1) * M:(at + 2) * M]
            out += lax.dot_general(table, zh, NT, preferred_element_type=F32)
            return out

        cz = three(0)
        sz = three(2)
        fre = cz[:, :128] - sz[:, 128:]
        fim = sz[:, :128] + cz[:, 128:]
        for d in range(count):
            fsend[d, 0, pl.ds(t, 16, stride=R), :] = fre[d * 16:(d + 1) * 16]
            fsend[d, 1, pl.ds(t, 16, stride=R), :] = fim[d * 16:(d + 1) * 16]
        return carry

    if LOOP_X:
        lax.fori_loop(0, R, stage_x, 0)
    else:
        for t in range(R):
            stage_x(t, 0)

    pl.semaphore_wait(barrier, count - 1)
    copies = []
    for k in SENDS:
        other = lax.rem(me // 4 + k // 4, 4) * 4 + jnp.bitwise_xor(lax.rem(me, 4), k % 4)
        copy = pltpu.make_async_remote_copy(
            src_ref=fsend.at[other],
            dst_ref=grecv.at[me],
            send_sem=send_sem.at[k],
            recv_sem=recv_sem.at[k],
            device_id={"gx": other},
            device_id_type=MESH,
        )
        copy.start()
        copies.append(copy)
    grecv[me] = fsend[me]
    loads[4].wait()
    for copy in copies:
        copy.wait()

    lane = lax.broadcasted_iota(jnp.int32, (16, 128), 1)
    for j in range(R):
        def cells_step(c, carry, j=j):
            row = pl.multiple_of(c * 16, 16)
            re = [grecv[R * s + j, 0, pl.ds(row, 16), :] for s in range(R)]
            im = [grecv[R * s + j, 1, pl.ds(row, 16), :] for s in range(R)]
            for t, (yr, yi) in enumerate(butterfly(re, im)):
                base = t * 2 * R + j
                wr = tw2[base:base + 1, :]
                if t:
                    wi = tw2[base + R:base + R + 1, :]
                    yr, yi = yr * wr - yi * wi, yr * wi + yi * wr
                else:
                    yr, yi = yr * wr, yi * wr
                for c_at, part in enumerate((yr, yi)):
                    for p in range(2):
                        mine = jnp.where((lane >= 64) == (p == 1), part, 0.0)
                        high, low = split(mine)
                        at = pl.ds(pl.multiple_of(t * 128 + p * 64 + row, 16), 16)
                        cols = slice((c_at * R + j) * 128, (c_at * R + j + 1) * 128)
                        z2h[at, cols] = high
                        z2l[at, cols] = low
            return carry
        lax.fori_loop(0, 4, cells_step, 0)

    for half in range(2):
        zh = z2h[half * 256:(half + 1) * 256, :]
        zl = z2l[half * 256:(half + 1) * 256, :]
        out = lax.dot_general(tabs[:M], zh, NT, preferred_element_type=F32)
        out += lax.dot_general(tabs[:M], zl, NT, preferred_element_type=F32)
        out += lax.dot_general(tabs[M:2 * M], zh, NT, preferred_element_type=F32)
        for i in range(2):
            yx[pl.ds(half * 2 + i, M, stride=R), :] = out[:, i * 128:(i + 1) * 128]
    for b in range(N // 128):
        tile = jnp.transpose(yx[b * 128:(b + 1) * 128, :])
        cols = slice(b * 128, (b + 1) * 128)
        pot[0, :, cols] = tile[:64]
        pot[1, :, cols] = tile[64:]
        total = tile[:64] + tile[64:]
        padded[b, 16:80, :] = total
        if b == 0:
            padded[N // 128, 16:80, :] = total

    left = lax.rem(me + count - 1, count)
    right = lax.rem(me + 1, count)
    to_left = pltpu.make_async_remote_copy(
        src_ref=padded.at[:, 16:32, :], dst_ref=padded.at[:, 80:96, :],
        send_sem=rim_send.at[0], recv_sem=rim_recv.at[0],
        device_id={"gx": left}, device_id_type=MESH,
    )
    to_right = pltpu.make_async_remote_copy(
        src_ref=padded.at[:, 64:80, :], dst_ref=padded.at[:, 0:16, :],
        send_sem=rim_send.at[1], recv_sem=rim_recv.at[1],
        device_id={"gx": right}, device_id_type=MESH,
    )
    to_left.start()
    to_right.start()
    to_left.wait()
    to_right.wait()


def pairs_kernel(
    cell_s, pair_s, padded, expo_t, pair_v, block_v, slot_v, gauss, pot, message, pot_out, rows, pot_sem
):
    store = pltpu.make_async_copy(pot, pot_out, pot_sem)
    store.start()
    lane = lax.broadcasted_iota(jnp.int32, (W, 128), 1)
    use_low = ((lane >> 5) & 1) == 1
    blank = jnp.zeros((W, 128), BF16)

    def several(step, carry):
        operands, scales = [], []
        for n in range(GROUP):
            tabs, cells = [], []
            for q in range(2):
                p = (step * GROUP + n) * 2 + q
                i = pair_s[0, p]
                j = pair_s[1, p]
                cy, cx = cell_s[0, i], cell_s[1, i]
                dy = ((cy - cell_s[0, j] + N // 2) & (N - 1)) - N // 2
                dx = cx - cell_s[1, j]
                start = (cy - W // 2) & (N - 1)
                tile = start >> 7
                off = start & 127
                turn = (-off) & 127
                low_part = pltpu.roll(padded[tile, pl.ds(cx, W), :], turn, 1)
                high_part = pltpu.roll(padded[tile + 1, pl.ds(cx, W), :], turn, 1)
                window = jnp.where(lane < 128 - off, low_part, high_part)
                window = jnp.where(lane < W, window, 0.0)
                window = window + pltpu.roll(window, 32, 1)
                window = window + pltpu.roll(window, 64, 1)
                high, low = split(window)
                both = jnp.where(use_low, low, high)
                cells.append(
                    jnp.concatenate([both, blank] if q == 0 else [blank, both], axis=1)
                )
                high, low = gauss[dy + SPAN // 2, :, :WIDE], gauss[dy + SPAN // 2, :, WIDE:2 * WIDE]
                tabs += [high, high, low, low]
                scales.append(dx + SPAN // 2)
            operands.append((jnp.concatenate(cells, axis=0), jnp.concatenate(tabs, axis=0)))
        done = []
        for n in range(GROUP):
            t = jnp.dot(*operands[n], preferred_element_type=F32)
            for q in range(2):
                at = scales[2 * n + q]
                high, low = gauss[at, :, 2 * WIDE:3 * WIDE], gauss[at, :, 3 * WIDE:]
                scaled = t[q * W:(q + 1) * W] * (high.astype(F32) + low.astype(F32))
                done.append(jnp.sum(scaled, axis=0, keepdims=True))
        at = pl.ds(pl.multiple_of(step * GROUP * 2, GROUP * 2), GROUP * 2)
        rows[at, :] = jnp.concatenate(done, axis=0)
        return carry

    lax.fori_loop(0, 64 // GROUP, several, 0)
    message[0:128, :] = jnp.transpose(rows[:, 0:128])
    message[128:ROWS, :] = jnp.transpose(rows[:, 128:256])[:ROWS - 128]

    sub = lax.broadcasted_iota(jnp.int32, (128, 128), 0)
    exps = expo_t[...].astype(F32).astype(BF16)
    for side in range(2):
        hot = jnp.where(pair_v[side:side + 1, :] == sub, 1.0, 0.0).astype(BF16)
        at = ROWS + 64 * side
        message[at:at + 64, :] = jnp.dot(exps, hot, preferred_element_type=F32)
    hot = jnp.where(block_v[...] == sub, 1.0, 0.0).astype(BF16)
    slots = jnp.broadcast_to(slot_v[...].astype(F32), (8, 128)).astype(BF16)
    message[ROWS + 128:MSG, :] = jnp.dot(slots, hot, preferred_element_type=F32)
    store.wait()


def reduce_kernel(
    message, out, theirs, bits, xsel, hits, ebuf, part0, part1, part2, near0, near1, near2,
    row0, row1, row2, far0, far1, far2,
    sm_sem, rm_sem, sb_sem, rb_sem, sc_sem, rc_sem,
):
    parts, nears, rows_of, fars = (
        (part0, part1, part2), (near0, near1, near2), (row0, row1, row2), (far0, far1, far2)
    )
    gx = lax.axis_index("gx")
    gy = lax.axis_index("gy")
    z, xh, core = gx // 4, lax.rem(gx // 2, 2), lax.rem(gx, 2)
    xl, y = gy // 4, lax.rem(gy, 4)
    x = xh * 2 + xl
    sibling = {"gx": z * 4 + xh * 2 + (1 - core), "gy": gy}

    def at(kz, ky, kx):
        to_x = lax.rem(x + kx, 4)
        to_gx = lax.rem(z + kz, 4) * 4 + (to_x // 2) * 2 + core
        return {"gx": to_gx, "gy": lax.rem(to_x, 2) * 4 + lax.rem(y + ky, 4)}

    axes = (("y", "z", "x"), ("z", "y", "x"), ("x", "z", "y"))
    place_of = {"z": z, "y": y, "x": x}

    def along(h, k0, k1, k2):
        step = dict(zip(axes[h], (k0, k1, k2)))
        return at(step["z"], step["y"], step["x"])

    barrier = pltpu.get_barrier_semaphore()
    partners = [sibling] + [
        at(kz, ky, kx)
        for kz in range(4) for ky in range(4) for kx in range(4)
        if 0 in (kz, ky, kx) and (kz, ky, kx) != (0, 0, 0)
    ]
    for device in partners:
        pl.semaphore_signal(barrier, inc=1, device_id=device, device_id_type=MESH)

    def send(src, dst, ssem, rsem, device):
        copy = pltpu.make_async_remote_copy(
            src_ref=src, dst_ref=dst, send_sem=ssem, recv_sem=rsem,
            device_id=device, device_id_type=MESH,
        )
        copy.start()
        return copy


    sub = lax.broadcasted_iota(jnp.int32, (64, 128), 0)

    def prepare(o, source):
        slot = source[ROWS + 128:ROWS + 129, :].astype(jnp.int32)
        where = {
            "z": slot >> 5, "x": ((slot >> 4) & 1) * 2 + ((slot >> 2) & 1), "y": slot & 3
        }
        kept = ((slot >> 3) & 1) == core
        for h in range(3):
            a, b, c = (where[axis] for axis in axes[h])
            place = jnp.where(kept, a * 16 + b * 4 + c, 64)
            hit = jnp.where(place == sub, 1.0, 0.0).astype(BF16)
            hits[h, :, o * 256:o * 256 + 128] = hit
            hits[h, :, o * 256 + 128:o * 256 + 256] = hit

        exponent = source[ROWS:ROWS + 64, :].astype(jnp.int32)
        for b in range(4):
            bits[o, b] = jnp.where((exponent & (1 << b)) != 0, 1.0, 0.0)

        def choose_second(c, carry):
            rows = pl.ds(pl.multiple_of(c * 16, 16), 16)
            mine = source[pl.ds(pl.multiple_of(ROWS + 64 + c * 16, 16), 16), :]
            masks = [mine == float(f) for f in range(1, NE)]
            for e in range(NE):
                got = jnp.broadcast_to(source[e * NE:e * NE + 1, :], (16, 128))
                for f in range(1, NE):
                    got = jnp.where(masks[f - 1], source[e * NE + f:e * NE + f + 1, :], got)
                xsel[o, 0, e, rows, :], xsel[o, 1, e, rows, :] = split(got)
            return carry

        lax.fori_loop(0, 4, choose_second, 0)

    def choose(o, start, steps, size):
        def rows_step(c, carry):
            rows = pl.ds(pl.multiple_of(c * 16, 16), 16)
            held = [[xsel[o, s, e, rows, :] for e in range(NE)] for s in range(2)]

            def choose_first(g, carry):
                first = start + g * size
                masks = [
                    [
                        jnp.broadcast_to(bits[o, b, pl.ds(first + k, 1), :], (16, 128)).astype(BF16) > 0.5
                        for b in range(4)
                    ]
                    for k in range(size)
                ]
                done = []
                for b0, b1, b2, b3 in masks:
                    for s in range(2):
                        got = held[s]
                        got = [jnp.where(b0, got[e + 1], got[e]) for e in range(0, NE, 2)]
                        got = [jnp.where(b1, got[e + 1], got[e]) for e in range(0, NE // 2, 2)]
                        done.append(jnp.where(b3, got[2], jnp.where(b2, got[1], got[0])))
                for k in range(size):
                    at = pl.ds(pl.multiple_of((first + k) * 64 + c * 16, 16), 16)
                    for s in range(2):
                        col = o * 256 + s * 128
                        ebuf[at, col:col + 128] = done[2 * k + s]
                return carry

            lax.fori_loop(0, steps, choose_first, 0)
            return carry

        lax.fori_loop(0, 4, rows_step, 0)

    prepare(0, message)
    choose(0, 0, 64 // STEP, STEP)
    pl.semaphore_wait(barrier, len(partners))
    swap = send(message, theirs, sm_sem.at[0], rm_sem.at[0], sibling)

    def slot_sum(h, o):
        k0, cols = sum(KS[:h]), slice(o * 256, o * 256 + 256)
        return lax.dot_general(
            hits[h, :, cols], ebuf[k0 * 64:(k0 + KS[h]) * 64, cols], NT,
            preferred_element_type=F32,
        )

    for h in range(3):
        got = slot_sum(h, 0)
        for a in range(4):
            parts[h][a] = got[a * 16:(a + 1) * 16]
    swap.wait_recv()
    prepare(1, theirs)
    second = {}
    for h in range(3):
        k0 = sum(KS[:h])
        choose(1, k0, KS[h] // SIZES[h], SIZES[h])
        got = slot_sum(h, 1)
        for a in range(4):
            parts[h][a] = parts[h][a] + got[a * 16:(a + 1) * 16]
        mine = place_of[axes[h][0]]
        for k in (2, 1, 3):
            second[h, k] = send(
                parts[h].at[lax.rem(mine + k, 4)], nears[h].at[k - 1],
                sb_sem.at[h, k], rb_sem.at[h, k], along(h, k, 0, 0),
            )
    third = {}
    for h in range(3):
        for k in (1, 3, 2):
            second[h, k].wait_recv()
        total = parts[h][place_of[axes[h][0]]] + nears[h][0] + nears[h][1] + nears[h][2]
        for c in range(KS[h] // 2):
            rows_of[h][:, c, :] = total[:, c * 128:(c + 1) * 128]
        b, c = (place_of[axis] for axis in axes[h][1:])
        for kb in (2, 1, 3, 0):
            for kc in (2, 1, 3, 0):
                if kb or kc:
                    to = lax.rem(b + kb, 4) * 4 + lax.rem(c + kc, 4)
                    at_k = kb * 4 + kc
                    third[h, at_k] = send(
                        rows_of[h].at[to], fars[h].at[at_k - 1],
                        sc_sem.at[h, at_k], rc_sem.at[h, at_k], along(h, 0, kb, kc),
                    )
    for h in range(3):
        b, c = (place_of[axis] for axis in axes[h][1:])
        done = rows_of[h][b * 4 + c]
        for at_k in range(1, 16):
            third[h, at_k].wait_recv()
        for at_k in range(1, 16):
            done = done + fars[h][at_k - 1]
        k0 = sum(KS[:h])
        out[0, pl.ds(k0, KS[h] // 2, stride=2), :] = done[:, :64]
        out[0, pl.ds(k0 + 1, KS[h] // 2, stride=2), :] = done[:, 64:]
    swap.wait_send()
    for group in (second, third):
        for copy in group.values():
            copy.wait_send()


def body(kpot, atom_cell, expo, pair_atoms, pair_block, block_slot):
    vmem = pl.BlockSpec(memory_space=pltpu.VMEM)
    smem = pl.BlockSpec(memory_space=pltpu.SMEM)
    dma = pltpu.SemaphoreType.DMA
    blob = jnp.asarray(transform_tables())
    gauss = jnp.asarray(gauss_tables())
    potential, padded = pl.pallas_call(
        transform_kernel,
        out_shape=(
            jax.ShapeDtypeStruct((2, CXL, N), F32),
            jax.ShapeDtypeStruct((N // 128 + 1, 96, 128), F32),
        ),
        in_specs=[pl.BlockSpec(memory_space=pl.ANY)] * 2,
        out_specs=(vmem, vmem),
        scratch_shapes=[
            pltpu.VMEM(kpot.shape, F32),
            pltpu.VMEM((USED, N), BF16),
            pltpu.VMEM((2 * R, M), F32),
            pltpu.VMEM((2 * R * R, 2 * CXL), F32),
            pltpu.VMEM((R, 256, M), BF16),
            pltpu.VMEM((R, 256, M), BF16),
            pltpu.VMEM((16, 2, CXL, 128), F32),
            pltpu.VMEM((16, 2, CXL, 128), F32),
            pltpu.VMEM((512, N), BF16),
            pltpu.VMEM((512, N), BF16),
            pltpu.VMEM((N, 128), F32),
            dma((5,)), dma((16,)), dma((16,)), dma((2,)), dma((2,)),
        ],
        compiler_params=pltpu.CompilerParams(
            collective_id=0, has_side_effects=True, vmem_limit_bytes=211 * 2**18
        ),
        name="transform",
    )(kpot, blob)
    cell_t, pair_t = atom_cell.T, pair_atoms.T
    message, potential = pl.pallas_call(
        pairs_kernel,
        out_shape=(
            jax.ShapeDtypeStruct((MSG, 128), F32), jax.ShapeDtypeStruct(potential.shape, F32)
        ),
        in_specs=[smem, smem] + [vmem] * 6 + [pl.BlockSpec(memory_space=pl.ANY)],
        out_specs=(vmem, pl.BlockSpec(memory_space=pl.ANY)),
        scratch_shapes=[pltpu.VMEM((128, WIDE), F32), dma],
        compiler_params=pltpu.CompilerParams(vmem_limit_bytes=16 * 2**20),
        name="pairs",
    )(
        cell_t, pair_t, padded, expo.T, pair_t,
        pair_block.reshape(1, -1), block_slot.reshape(1, -1), gauss, potential,
    )
    units = [k // 2 for k in KS]
    own = pl.pallas_call(
        reduce_kernel,
        out_shape=jax.ShapeDtypeStruct((1, 64, 64), F32),
        in_specs=[vmem],
        out_specs=vmem,
        scratch_shapes=[
            pltpu.VMEM((MSG, 128), F32),
            pltpu.VMEM((2, 4, 64, 128), F32),
            pltpu.VMEM((2, 2, NE, 64, 128), BF16),
            pltpu.VMEM((3, 64, 512), BF16),
            pltpu.VMEM((4096, 512), BF16),
        ]
        + [pltpu.VMEM((4, 16, u * 128), F32) for u in units]
        + [pltpu.VMEM((3, 16, u * 128), F32) for u in units]
        + [pltpu.VMEM((16, u, 128), F32) for u in units]
        + [pltpu.VMEM((15, u, 128), F32) for u in units]
        + [dma((1,)), dma((1,)), dma((3, 4)), dma((3, 4)), dma((3, 16)), dma((3, 16))],
        compiler_params=pltpu.CompilerParams(
            collective_id=1, has_side_effects=True, vmem_limit_bytes=24 * 2**20
        ),
        name="reduce",
    )(message)
    return jnp.transpose(potential, (0, 2, 1)), own


def solution(mesh):
    return jax.shard_map(
        body,
        mesh=mesh,
        in_specs=(
            P(None, "gy", "gx", None),
            P(("gx", "gy"), None),
            P(("gx", "gy"), None),
            P(("gx", "gy"), None),
            P(("gx", "gy")),
            P(),
        ),
        out_specs=(P("gy", None, "gx"), P(("gx", "gy"), None, None)),
        check_vma=False,
    )
```

```python
import math

import jax
import jax.numpy as jnp
import ml_dtypes
import numpy as np
from jax import lax
from jax.experimental import pallas as pl
from jax.experimental.pallas import tpu as pltpu
from jax.sharding import PartitionSpec as P

W = 32
NE = 12
ROWS = NE * NE
WIDE = 256
SPAN = 33
N = 1024
R = 4
M = N // R
CXL = 64
KS = (24, 22, 18)
SIZES = (8, 11, 9)
STEP = 8
MSG = 280
SENDS = (10, 11, 8, 9, 6, 7, 4, 5, 14, 15, 12, 13, 2, 3, 1)
LOOP_X = False
GROUP = 16
BLOB = 4096
USED = 816
MESH = pl.DeviceIdType.MESH
NT = (((1,), (1,)), ((), ()))
F32 = jnp.float32
BF16 = jnp.bfloat16


def split_np(values):
    high = values.astype(np.float32).astype(ml_dtypes.bfloat16)
    low = (values - high.astype(np.float64)).astype(np.float32).astype(ml_dtypes.bfloat16)
    return high, low


def split(values):
    high = values.astype(BF16)
    low = (values - high.astype(F32)).astype(BF16)
    return high, low


def transform_tables():
    n = np.arange(M)
    angle = 2.0 * math.pi / M * ((n[:, None] * n[None, :]) % M)
    cos, sin = np.cos(angle), np.sin(angle)
    tab1 = np.stack([*split_np(cos), *split_np(sin)])
    def spread(t):
        t = t.reshape(M, R, CXL)
        return np.stack([t, t], axis=2).reshape(M, 2 * M)

    tab2 = np.stack(split_np(np.concatenate([spread(cos), -spread(sin)], axis=1)))
    t = np.arange(R)
    turn = 2.0 * math.pi / N * (t[:, None] * n[None, :])
    tw1 = np.stack([np.cos(turn), np.sin(turn)], axis=1).astype(np.float32).reshape(2 * R, M)
    scale = 1.0 / (N * N)
    tw2 = np.stack([np.cos(turn), np.sin(turn)], axis=1) * scale
    tw2 = tw2.reshape(R, 2, R, 1, CXL)
    tw2 = np.broadcast_to(tw2, (R, 2, R, 2, CXL)).astype(np.float32).reshape(R * 2 * R, 2 * CXL)

    def three(turns):
        high = turns.astype(ml_dtypes.bfloat16)
        mid = (turns - high.astype(np.float32)).astype(ml_dtypes.bfloat16)
        low = (turns - high.astype(np.float32) - mid.astype(np.float32)).astype(ml_dtypes.bfloat16)
        return np.concatenate([high, mid, low], axis=1)

    blob = np.zeros((BLOB, N), ml_dtypes.bfloat16)
    blob[:512] = tab2.reshape(512, N)
    blob[512:768] = tab1.transpose(1, 0, 2).reshape(M, N)
    blob[768:768 + 2 * R, :3 * M] = three(tw1)
    blob[784:784 + 2 * R * R, :6 * CXL] = three(tw2)
    return blob


def gauss_tables():
    alpha = (2.0 / (W * W)) * 16.0 ** (np.arange(NE) / (NE - 1))
    offs = np.arange(W) - W // 2
    shift = np.arange(SPAN) - SPAN // 2
    e = alpha[None, :, None, None] * (offs**2)[None, None, None, :]
    f = alpha[None, None, :, None] * ((offs[None, :] + shift[:, None]) ** 2)[:, None, None, :]
    grid = np.exp(-(e + f)).reshape(SPAN, ROWS, W).transpose(0, 2, 1)
    grid = np.concatenate([grid, np.zeros((SPAN, W, WIDE - ROWS))], axis=2)
    depth = np.zeros(WIDE)
    depth[:ROWS] = np.exp(-(alpha[:, None] + alpha[None, :]) * 0.25).reshape(-1) / W
    return np.concatenate([*split_np(grid), *split_np(grid * depth)], axis=2)


def butterfly(re, im):
    ar, br, cr, dr = re[0] + re[2], re[0] - re[2], re[1] + re[3], re[1] - re[3]
    ai, bi, ci, di = im[0] + im[2], im[0] - im[2], im[1] + im[3], im[1] - im[3]
    return (
        (ar + cr, ai + ci),
        (br - di, bi + dr),
        (ar - cr, ai - ci),
        (br + di, bi - dr),
    )


def transform_kernel(
    kpot_any, blob, pot, padded, kpot, tabs, tw1, tw2, z1h, z1l, fsend, grecv, z2h, z2l, yx,
    load_sem, send_sem, recv_sem, rim_send, rim_recv,
):
    moves = (
        (kpot_any.at[:, 0], kpot.at[:, 0]),
        (blob.at[768:USED], tabs.at[768:USED]),
        (kpot_any.at[:, 1], kpot.at[:, 1]),
        (blob.at[512:768], tabs.at[512:768]),
        (blob.at[0:512], tabs.at[0:512]),
    )
    loads = [
        pltpu.make_async_copy(source, target, load_sem.at[i])
        for i, (source, target) in enumerate(moves)
    ]
    for load in loads:
        load.start()
    me = lax.axis_index("gx")
    count = 16
    barrier = pltpu.get_barrier_semaphore()
    for k in range(1, count):
        pl.semaphore_signal(
            barrier, inc=1, device_id={"gx": lax.rem(me + k, count)}, device_id_type=MESH
        )

    loads[1].wait()
    turns = tabs[768:784, :3 * M].astype(F32)
    tw1[...] = (turns[:, :M] + turns[:, M:2 * M] + turns[:, 2 * M:])[:2 * R]
    turns = tabs[784:816, :6 * CXL].astype(F32)
    tw2[...] = turns[:, :128] + turns[:, 128:256] + turns[:, 256:]
    for p in range(2):
        loads[2 * p].wait()

        def rows_step(c, carry, p=p):
            row = pl.multiple_of(c * 16, 16)
            re = [kpot[0, p, pl.ds(row, 16), s * M:(s + 1) * M] for s in range(R)]
            im = [kpot[1, p, pl.ds(row, 16), s * M:(s + 1) * M] for s in range(R)]
            for t, (yr, yi) in enumerate(butterfly(re, im)):
                if t:
                    wr = tw1[2 * t:2 * t + 1, :]
                    wi = tw1[2 * t + 1:2 * t + 2, :]
                    yr, yi = yr * wr - yi * wi, yr * wi + yi * wr
                for c_at, part in enumerate((yr, yi)):
                    high, low = split(part)
                    at = pl.ds(pl.multiple_of(c_at * 128 + p * 64 + row, 16), 16)
                    z1h[t, at, :] = high
                    z1l[t, at, :] = low
            return carry
        lax.fori_loop(0, 4, rows_step, 0)

    loads[3].wait()

    def stage_x(t, carry):
        zh, zl = z1h[t], z1l[t]

        def three(at):
            table = tabs[512:768, at * M:(at + 1) * M]
            out = lax.dot_general(table, zh, NT, preferred_element_type=F32)
            out += lax.dot_general(table, zl, NT, preferred_element_type=F32)
            table = tabs[512:768, (at + 1) * M:(at + 2) * M]
            out += lax.dot_general(table, zh, NT, preferred_element_type=F32)
            return out

        cz = three(0)
        sz = three(2)
        fre = cz[:, :128] - sz[:, 128:]
        fim = sz[:, :128] + cz[:, 128:]
        for d in range(count):
            fsend[d, 0, pl.ds(t, 16, stride=R), :] = fre[d * 16:(d + 1) * 16]
            fsend[d, 1, pl.ds(t, 16, stride=R), :] = fim[d * 16:(d + 1) * 16]
        return carry

    if LOOP_X:
        lax.fori_loop(0, R, stage_x, 0)
    else:
        for t in range(R):
            stage_x(t, 0)

    pl.semaphore_wait(barrier, count - 1)
    copies = []
    for k in SENDS:
        other = lax.rem(me // 4 + k // 4, 4) * 4 + jnp.bitwise_xor(lax.rem(me, 4), k % 4)
        copy = pltpu.make_async_remote_copy(
            src_ref=fsend.at[other],
            dst_ref=grecv.at[me],
            send_sem=send_sem.at[k],
            recv_sem=recv_sem.at[k],
            device_id={"gx": other},
            device_id_type=MESH,
        )
        copy.start()
        copies.append(copy)
    grecv[me] = fsend[me]
    loads[4].wait()
    for copy in copies:
        copy.wait()

    lane = lax.broadcasted_iota(jnp.int32, (16, 128), 1)
    for j in range(R):
        def cells_step(c, carry, j=j):
            row = pl.multiple_of(c * 16, 16)
            re = [grecv[R * s + j, 0, pl.ds(row, 16), :] for s in range(R)]
            im = [grecv[R * s + j, 1, pl.ds(row, 16), :] for s in range(R)]
            for t, (yr, yi) in enumerate(butterfly(re, im)):
                base = t * 2 * R + j
                wr = tw2[base:base + 1, :]
                if t:
                    wi = tw2[base + R:base + R + 1, :]
                    yr, yi = yr * wr - yi * wi, yr * wi + yi * wr
                else:
                    yr, yi = yr * wr, yi * wr
                for c_at, part in enumerate((yr, yi)):
                    for p in range(2):
                        mine = jnp.where((lane >= 64) == (p == 1), part, 0.0)
                        high, low = split(mine)
                        at = pl.ds(pl.multiple_of(t * 128 + p * 64 + row, 16), 16)
                        cols = slice((c_at * R + j) * 128, (c_at * R + j + 1) * 128)
                        z2h[at, cols] = high
                        z2l[at, cols] = low
            return carry
        lax.fori_loop(0, 4, cells_step, 0)

    for half in range(2):
        zh = z2h[half * 256:(half + 1) * 256, :]
        zl = z2l[half * 256:(half + 1) * 256, :]
        out = lax.dot_general(tabs[:M], zh, NT, preferred_element_type=F32)
        out += lax.dot_general(tabs[:M], zl, NT, preferred_element_type=F32)
        out += lax.dot_general(tabs[M:2 * M], zh, NT, preferred_element_type=F32)
        for i in range(2):
            yx[pl.ds(half * 2 + i, M, stride=R), :] = out[:, i * 128:(i + 1) * 128]
    for b in range(N // 128):
        tile = jnp.transpose(yx[b * 128:(b + 1) * 128, :])
        cols = slice(b * 128, (b + 1) * 128)
        pot[0, :, cols] = tile[:64]
        pot[1, :, cols] = tile[64:]
        total = tile[:64] + tile[64:]
        padded[b, 16:80, :] = total
        if b == 0:
            padded[N // 128, 16:80, :] = total

    left = lax.rem(me + count - 1, count)
    right = lax.rem(me + 1, count)
    to_left = pltpu.make_async_remote_copy(
        src_ref=padded.at[0:8, 16:32, :], dst_ref=padded.at[0:8, 80:96, :],
        send_sem=rim_send.at[0], recv_sem=rim_recv.at[0],
        device_id={"gx": left}, device_id_type=MESH,
    )
    to_right = pltpu.make_async_remote_copy(
        src_ref=padded.at[0:8, 64:80, :], dst_ref=padded.at[0:8, 0:16, :],
        send_sem=rim_send.at[1], recv_sem=rim_recv.at[1],
        device_id={"gx": right}, device_id_type=MESH,
    )
    to_left.start()
    to_right.start()
    to_left.wait()
    to_right.wait()
    for rows in (slice(0, 16), slice(80, 96)):
        padded[N // 128, rows, :] = padded[0, rows, :]


def pairs_kernel(
    cell_s, pair_s, padded, expo_t, pair_v, block_v, slot_v, gauss, pot, message, pot_out, rows, pot_sem
):
    store = pltpu.make_async_copy(pot, pot_out, pot_sem)
    store.start()
    lane = lax.broadcasted_iota(jnp.int32, (W, 128), 1)
    use_low = ((lane >> 5) & 1) == 1
    blank = jnp.zeros((W, 128), BF16)

    def several(step, carry):
        operands, scales = [], []
        for n in range(GROUP):
            tabs, cells = [], []
            for q in range(2):
                p = (step * GROUP + n) * 2 + q
                i = pair_s[0, p]
                j = pair_s[1, p]
                cy, cx = cell_s[0, i], cell_s[1, i]
                dy = ((cy - cell_s[0, j] + N // 2) & (N - 1)) - N // 2
                dx = cx - cell_s[1, j]
                start = (cy - W // 2) & (N - 1)
                tile = start >> 7
                off = start & 127
                turn = (-off) & 127
                low_part = pltpu.roll(padded[tile, pl.ds(cx, W), :], turn, 1)
                high_part = pltpu.roll(padded[tile + 1, pl.ds(cx, W), :], turn, 1)
                window = jnp.where(lane < 128 - off, low_part, high_part)
                window = jnp.where(lane < W, window, 0.0)
                window = window + pltpu.roll(window, 32, 1)
                window = window + pltpu.roll(window, 64, 1)
                high, low = split(window)
                both = jnp.where(use_low, low, high)
                cells.append(
                    jnp.concatenate([both, blank] if q == 0 else [blank, both], axis=1)
                )
                high, low = gauss[dy + SPAN // 2, :, :WIDE], gauss[dy + SPAN // 2, :, WIDE:2 * WIDE]
                tabs += [high, high, low, low]
                scales.append(dx + SPAN // 2)
            operands.append((jnp.concatenate(cells, axis=0), jnp.concatenate(tabs, axis=0)))
        done = []
        for n in range(GROUP):
            t = jnp.dot(*operands[n], preferred_element_type=F32)
            for q in range(2):
                at = scales[2 * n + q]
                high, low = gauss[at, :, 2 * WIDE:3 * WIDE], gauss[at, :, 3 * WIDE:]
                scaled = t[q * W:(q + 1) * W] * (high.astype(F32) + low.astype(F32))
                done.append(jnp.sum(scaled, axis=0, keepdims=True))
        at = pl.ds(pl.multiple_of(step * GROUP * 2, GROUP * 2), GROUP * 2)
        rows[at, :] = jnp.concatenate(done, axis=0)
        return carry

    lax.fori_loop(0, 64 // GROUP, several, 0)
    message[0:128, :] = jnp.transpose(rows[:, 0:128])
    message[128:ROWS, :] = jnp.transpose(rows[:, 128:256])[:ROWS - 128]

    sub = lax.broadcasted_iota(jnp.int32, (128, 128), 0)
    exps = expo_t[...].astype(F32).astype(BF16)
    for side in range(2):
        hot = jnp.where(pair_v[side:side + 1, :] == sub, 1.0, 0.0).astype(BF16)
        at = ROWS + 64 * side
        message[at:at + 64, :] = jnp.dot(exps, hot, preferred_element_type=F32)
    hot = jnp.where(block_v[...] == sub, 1.0, 0.0).astype(BF16)
    slots = jnp.broadcast_to(slot_v[...].astype(F32), (8, 128)).astype(BF16)
    message[ROWS + 128:MSG, :] = jnp.dot(slots, hot, preferred_element_type=F32)
    store.wait()


def reduce_kernel(
    message, out, theirs, bits, xsel, hits, ebuf, part0, part1, part2, near0, near1, near2,
    row0, row1, row2, far0, far1, far2,
    sm_sem, rm_sem, sb_sem, rb_sem, sc_sem, rc_sem,
):
    parts, nears, rows_of, fars = (
        (part0, part1, part2), (near0, near1, near2), (row0, row1, row2), (far0, far1, far2)
    )
    gx = lax.axis_index("gx")
    gy = lax.axis_index("gy")
    z, xh, core = gx // 4, lax.rem(gx // 2, 2), lax.rem(gx, 2)
    xl, y = gy // 4, lax.rem(gy, 4)
    x = xh * 2 + xl
    sibling = {"gx": z * 4 + xh * 2 + (1 - core), "gy": gy}

    def at(kz, ky, kx):
        to_x = lax.rem(x + kx, 4)
        to_gx = lax.rem(z + kz, 4) * 4 + (to_x // 2) * 2 + core
        return {"gx": to_gx, "gy": lax.rem(to_x, 2) * 4 + lax.rem(y + ky, 4)}

    axes = (("y", "z", "x"), ("z", "y", "x"), ("x", "z", "y"))
    place_of = {"z": z, "y": y, "x": x}

    def along(h, k0, k1, k2):
        step = dict(zip(axes[h], (k0, k1, k2)))
        return at(step["z"], step["y"], step["x"])

    barrier = pltpu.get_barrier_semaphore()
    partners = [sibling] + [
        at(kz, ky, kx)
        for kz in range(4) for ky in range(4) for kx in range(4)
        if 0 in (kz, ky, kx) and (kz, ky, kx) != (0, 0, 0)
    ]
    for device in partners:
        pl.semaphore_signal(barrier, inc=1, device_id=device, device_id_type=MESH)

    def send(src, dst, ssem, rsem, device):
        copy = pltpu.make_async_remote_copy(
            src_ref=src, dst_ref=dst, send_sem=ssem, recv_sem=rsem,
            device_id=device, device_id_type=MESH,
        )
        copy.start()
        return copy


    sub = lax.broadcasted_iota(jnp.int32, (64, 128), 0)

    def prepare(o, source):
        slot = source[ROWS + 128:ROWS + 129, :].astype(jnp.int32)
        where = {
            "z": slot >> 5, "x": ((slot >> 4) & 1) * 2 + ((slot >> 2) & 1), "y": slot & 3
        }
        kept = ((slot >> 3) & 1) == core
        for h in range(3):
            a, b, c = (where[axis] for axis in axes[h])
            place = jnp.where(kept, a * 16 + b * 4 + c, 64)
            hit = jnp.where(place == sub, 1.0, 0.0).astype(BF16)
            hits[h, :, o * 256:o * 256 + 128] = hit
            hits[h, :, o * 256 + 128:o * 256 + 256] = hit

        exponent = source[ROWS:ROWS + 64, :].astype(jnp.int32)
        for b in range(4):
            bits[o, b] = jnp.where((exponent & (1 << b)) != 0, 1.0, 0.0)

        def choose_second(c, carry):
            rows = pl.ds(pl.multiple_of(c * 16, 16), 16)
            mine = source[pl.ds(pl.multiple_of(ROWS + 64 + c * 16, 16), 16), :]
            masks = [mine == float(f) for f in range(1, NE)]
            for e in range(NE):
                got = jnp.broadcast_to(source[e * NE:e * NE + 1, :], (16, 128))
                for f in range(1, NE):
                    got = jnp.where(masks[f - 1], source[e * NE + f:e * NE + f + 1, :], got)
                xsel[o, 0, e, rows, :], xsel[o, 1, e, rows, :] = split(got)
            return carry

        lax.fori_loop(0, 4, choose_second, 0)

    def choose(o, start, steps, size):
        def rows_step(c, carry):
            rows = pl.ds(pl.multiple_of(c * 16, 16), 16)
            held = [[xsel[o, s, e, rows, :] for e in range(NE)] for s in range(2)]

            def choose_first(g, carry):
                first = start + g * size
                masks = [
                    [
                        jnp.broadcast_to(bits[o, b, pl.ds(first + k, 1), :], (16, 128)).astype(BF16) > 0.5
                        for b in range(4)
                    ]
                    for k in range(size)
                ]
                done = []
                for b0, b1, b2, b3 in masks:
                    for s in range(2):
                        got = held[s]
                        got = [jnp.where(b0, got[e + 1], got[e]) for e in range(0, NE, 2)]
                        got = [jnp.where(b1, got[e + 1], got[e]) for e in range(0, NE // 2, 2)]
                        done.append(jnp.where(b3, got[2], jnp.where(b2, got[1], got[0])))
                for k in range(size):
                    at = pl.ds(pl.multiple_of((first + k) * 64 + c * 16, 16), 16)
                    for s in range(2):
                        col = o * 256 + s * 128
                        ebuf[at, col:col + 128] = done[2 * k + s]
                return carry

            lax.fori_loop(0, steps, choose_first, 0)
            return carry

        lax.fori_loop(0, 4, rows_step, 0)

    prepare(0, message)
    choose(0, 0, 64 // STEP, STEP)
    pl.semaphore_wait(barrier, len(partners))
    swap = send(message, theirs, sm_sem.at[0], rm_sem.at[0], sibling)

    def slot_sum(h, o):
        k0, cols = sum(KS[:h]), slice(o * 256, o * 256 + 256)
        return lax.dot_general(
            hits[h, :, cols], ebuf[k0 * 64:(k0 + KS[h]) * 64, cols], NT,
            preferred_element_type=F32,
        )

    for h in range(3):
        got = slot_sum(h, 0)
        for a in range(4):
            parts[h][a] = got[a * 16:(a + 1) * 16]
    swap.wait_recv()
    prepare(1, theirs)
    second = {}
    for h in range(3):
        k0 = sum(KS[:h])
        choose(1, k0, KS[h] // SIZES[h], SIZES[h])
        got = slot_sum(h, 1)
        for a in range(4):
            parts[h][a] = parts[h][a] + got[a * 16:(a + 1) * 16]
        mine = place_of[axes[h][0]]
        for k in (2, 1, 3):
            second[h, k] = send(
                parts[h].at[lax.rem(mine + k, 4)], nears[h].at[k - 1],
                sb_sem.at[h, k], rb_sem.at[h, k], along(h, k, 0, 0),
            )
    third = {}
    for h in range(3):
        for k in (1, 3, 2):
            second[h, k].wait_recv()
        total = parts[h][place_of[axes[h][0]]] + nears[h][0] + nears[h][1] + nears[h][2]
        for c in range(KS[h] // 2):
            rows_of[h][:, c, :] = total[:, c * 128:(c + 1) * 128]
        b, c = (place_of[axis] for axis in axes[h][1:])
        for kb in (2, 1, 3, 0):
            for kc in (2, 1, 3, 0):
                if kb or kc:
                    to = lax.rem(b + kb, 4) * 4 + lax.rem(c + kc, 4)
                    at_k = kb * 4 + kc
                    third[h, at_k] = send(
                        rows_of[h].at[to], fars[h].at[at_k - 1],
                        sc_sem.at[h, at_k], rc_sem.at[h, at_k], along(h, 0, kb, kc),
                    )
    for h in range(3):
        b, c = (place_of[axis] for axis in axes[h][1:])
        done = rows_of[h][b * 4 + c]
        for at_k in range(1, 16):
            third[h, at_k].wait_recv()
        for at_k in range(1, 16):
            done = done + fars[h][at_k - 1]
        k0 = sum(KS[:h])
        out[0, pl.ds(k0, KS[h] // 2, stride=2), :] = done[:, :64]
        out[0, pl.ds(k0 + 1, KS[h] // 2, stride=2), :] = done[:, 64:]
    swap.wait_send()
    for group in (second, third):
        for copy in group.values():
            copy.wait_send()


def body(kpot, atom_cell, expo, pair_atoms, pair_block, block_slot):
    vmem = pl.BlockSpec(memory_space=pltpu.VMEM)
    smem = pl.BlockSpec(memory_space=pltpu.SMEM)
    dma = pltpu.SemaphoreType.DMA
    blob = jnp.asarray(transform_tables())
    gauss = jnp.asarray(gauss_tables())
    potential, padded = pl.pallas_call(
        transform_kernel,
        out_shape=(
            jax.ShapeDtypeStruct((2, CXL, N), F32),
            jax.ShapeDtypeStruct((N // 128 + 1, 96, 128), F32),
        ),
        in_specs=[pl.BlockSpec(memory_space=pl.ANY)] * 2,
        out_specs=(vmem, vmem),
        scratch_shapes=[
            pltpu.VMEM(kpot.shape, F32),
            pltpu.VMEM((USED, N), BF16),
            pltpu.VMEM((2 * R, M), F32),
            pltpu.VMEM((2 * R * R, 2 * CXL), F32),
            pltpu.VMEM((R, 256, M), BF16),
            pltpu.VMEM((R, 256, M), BF16),
            pltpu.VMEM((16, 2, CXL, 128), F32),
            pltpu.VMEM((16, 2, CXL, 128), F32),
            pltpu.VMEM((512, N), BF16),
            pltpu.VMEM((512, N), BF16),
            pltpu.VMEM((N, 128), F32),
            dma((5,)), dma((16,)), dma((16,)), dma((2,)), dma((2,)),
        ],
        compiler_params=pltpu.CompilerParams(
            collective_id=0, has_side_effects=True, vmem_limit_bytes=211 * 2**18
        ),
        name="transform",
    )(kpot, blob)
    cell_t, pair_t = atom_cell.T, pair_atoms.T
    message, potential = pl.pallas_call(
        pairs_kernel,
        out_shape=(
            jax.ShapeDtypeStruct((MSG, 128), F32), jax.ShapeDtypeStruct(potential.shape, F32)
        ),
        in_specs=[smem, smem] + [vmem] * 6 + [pl.BlockSpec(memory_space=pl.ANY)],
        out_specs=(vmem, pl.BlockSpec(memory_space=pl.ANY)),
        scratch_shapes=[pltpu.VMEM((128, WIDE), F32), dma],
        compiler_params=pltpu.CompilerParams(vmem_limit_bytes=16 * 2**20),
        name="pairs",
    )(
        cell_t, pair_t, padded, expo.T, pair_t,
        pair_block.reshape(1, -1), block_slot.reshape(1, -1), gauss, potential,
    )
    units = [k // 2 for k in KS]
    own = pl.pallas_call(
        reduce_kernel,
        out_shape=jax.ShapeDtypeStruct((1, 64, 64), F32),
        in_specs=[vmem],
        out_specs=vmem,
        scratch_shapes=[
            pltpu.VMEM((MSG, 128), F32),
            pltpu.VMEM((2, 4, 64, 128), F32),
            pltpu.VMEM((2, 2, NE, 64, 128), BF16),
            pltpu.VMEM((3, 64, 512), BF16),
            pltpu.VMEM((4096, 512), BF16),
        ]
        + [pltpu.VMEM((4, 16, u * 128), F32) for u in units]
        + [pltpu.VMEM((3, 16, u * 128), F32) for u in units]
        + [pltpu.VMEM((16, u, 128), F32) for u in units]
        + [pltpu.VMEM((15, u, 128), F32) for u in units]
        + [dma((1,)), dma((1,)), dma((3, 4)), dma((3, 4)), dma((3, 16)), dma((3, 16))],
        compiler_params=pltpu.CompilerParams(
            collective_id=1, has_side_effects=True, vmem_limit_bytes=24 * 2**20
        ),
        name="reduce",
    )(message)
    return jnp.transpose(potential, (0, 2, 1)), own


def solution(mesh):
    return jax.shard_map(
        body,
        mesh=mesh,
        in_specs=(
            P(None, "gy", "gx", None),
            P(("gx", "gy"), None),
            P(("gx", "gy"), None),
            P(("gx", "gy"), None),
            P(("gx", "gy")),
            P(),
        ),
        out_specs=(P("gy", None, "gx"), P(("gx", "gy"), None, None)),
        check_vma=False,
    )
```
